128 devices in a mesh: blk: 8 (over y, x_lo), grp: 16 (over z, x_hi, core).
Axes of the slice: x: 4 (x_hi: 2, x_lo: 2; x = x_hi * 2 + x_lo), y: 4, z: 4, core: 2. Of those that a mesh axis runs over, the one named last changes fastest.
Arguments:
- b_rows: bfloat16 [5120, 8, 896], P('grp', 'blk'), may hold values from -0.796875 to 0.796875
- aux_count: int32 [16], P('grp'), may hold values from 1 to 320, 5000 in all
- occ_pick: int32 [8], replicated, may hold values from 0 to 99, as said below
- eps_occ: float32 [100], replicated, may hold values from -2 to -0.5
- eps_vir: float32 [896], replicated, may hold values from 0.2 to 4
Outputs:
- gamma: bfloat16 [5120, 8, 896], P('grp', 'blk')
The draws below stay inside these ranges and needn't reach their ends.
Inputs may be any that keep to these rules, and one draw needn't show every extreme that they name: `aux_count`: the counts sum to 5000. `occ_pick`: distinct entries; 0 and 99 both appear.
All inputs are finite; a program needn't handle non-finite values. No bound on the sum of `aux_count` on one device may be relied on, other than what follows from the above.
Results may differ from the reference program's by a relative error of at most 0.015.
Values may be sent and summed in bfloat16 or wider, within the bound.
A program may use at most 64 MiB of HBM per device.

```python
import math
import jax
import jax.numpy as jnp
import numpy as np
from jax import lax

NOCC = 100
NVIR = 896
AUX_DEV = 320
OCC = 8
NAUX = 5120
N_GRP = 16


def draw_occ_pick(key, part):
    key = jax.random.fold_in(key, 5)
    first_key, second_key = jax.random.split(key)
    middle = jax.random.permutation(first_key, NOCC - 2)[:OCC - 2] + 1
    picks = jnp.concatenate([jnp.array([0, NOCC - 1], jnp.int32), middle.astype(jnp.int32)])
    return jax.random.permutation(second_key, picks).astype(jnp.int32)


def level_of(key, dims, cuts, low, largest):
    def one(axis_at, blocks):
        draws = jax.random.uniform(jax.random.fold_in(jax.random.fold_in(key, 6), axis_at), (blocks,), jnp.float32, low / len(cuts), largest / len(cuts))
        return jnp.repeat(jnp.exp(draws), dims[axis_at] // blocks).reshape((-1,) + (1,) * (len(dims) - axis_at - 1))

    loudness = one(*cuts[0])
    for cut in cuts[1:]:
        loudness = loudness * one(*cut)
    return loudness


def split_up(amount, total, reach, lean):
    weights = [(1 << 20) // math.isqrt(grade ** lean) + 1 for grade in range(2, amount + 1)]
    rest, counts = total - reach - (amount - 1), [1] * (amount - 1)
    while rest > 0:
        free = [i for i in range(amount - 1) if counts[i] < reach]
        pool, remaining = sum([weights[i] for i in free]), rest
        for i in free:
            extra = min(reach - counts[i], max(1, remaining * weights[i] // pool), rest)
            counts[i] = counts[i] + extra
            rest = rest - extra
    return np.array([reach] + counts)


def ragged(own_key, amount, total, bound, skew):
    if amount == 2:
        one = jax.random.randint(own_key, (), max(1, total - bound), min(bound, total - 1) + 1)
        return jnp.stack([one, total - one])
    tallies = jnp.asarray(split_up(amount, total, bound, skew), jnp.int32)
    twos = (amount - 1) // 2
    source_of, taker = tallies[1:1 + 2 * twos:2], tallies[2:2 + 2 * twos:2]
    margin = jnp.minimum(source_of - 1, bound - taker)
    passed = jax.random.randint(jax.random.fold_in(own_key, 1), (twos,), 0, 1 << 20) % (margin + 1)
    tallies = tallies.at[1:1 + 2 * twos:2].set(source_of - passed).at[2:2 + 2 * twos:2].set(taker + passed)
    return tallies[jax.random.permutation(jax.random.fold_in(own_key, 2), amount)]


def bell_draw(key, dims, width, bound, pieces=(), held_as=jnp.bfloat16):
    factor_of = level_of(key, dims, pieces, -0.22, 0.18) if pieces else 1.0
    values = jax.random.normal(key, dims, jnp.float32) * width * factor_of
    return jnp.minimum(jnp.maximum(values, -bound), bound).astype(held_as)


def setup_inputs(seed: int = 0) -> dict:
    keys = jax.random.split(jax.random.key(seed), 6)
    b_rows = bell_draw(keys[0], (NAUX, OCC, NVIR), 0.1, 0.796875, ((0, 16), (1, 8)))
    aux_count = ragged(keys[1], N_GRP, AUX_DEV * N_GRP * 125 // 128, AUX_DEV, 0).astype(jnp.int32)
    occ_pick = draw_occ_pick(jax.random.fold_in(keys[5], 71), 0)
    eps_occ = jnp.clip(jax.random.uniform(keys[3], (NOCC,), jnp.float32, -2.0, -0.5), -2.0, -0.5)
    eps_vir = jnp.clip(jax.random.uniform(keys[4], (NVIR,), jnp.float32, 0.2, 4.0), 0.2, 4.0)
    return {"b_rows": b_rows, "aux_count": aux_count, "occ_pick": occ_pick, "eps_occ": eps_occ, "eps_vir": eps_vir}


def reference(b_rows, aux_count, occ_pick, eps_occ, eps_vir):
    row_index = jnp.arange(NAUX, dtype=jnp.int32)
    owner = row_index // AUX_DEV
    alive = (row_index % AUX_DEV) < aux_count[owner]
    masked = jnp.where(alive[:, None, None], b_rows, jnp.zeros_like(b_rows))
    widened = masked.astype(jnp.float32)
    picked = eps_occ[occ_pick]

    def for_orbital(first):
        left = lax.dynamic_index_in_dim(widened, first, 1, keepdims=False)
        left_groups = left.reshape(N_GRP, AUX_DEV, NVIR)

        def for_partner(running, second):
            right = lax.dynamic_index_in_dim(widened, second, 1, keepdims=False)
            partials = jnp.einsum("gpa,gpb->gab", left_groups, right.reshape(N_GRP, AUX_DEV, NVIR))
            rounded = lax.optimization_barrier(partials.astype(jnp.bfloat16)).astype(jnp.float32)
            integral = jnp.sum(rounded, axis=0).astype(jnp.bfloat16)
            full_pair = lax.optimization_barrier(integral).astype(jnp.float32)
            energy_gap = picked[first] + picked[second] - eps_vir[:, None] - eps_vir[None, :]
            amplitude = ((2.0 * full_pair - full_pair.T) / energy_gap).astype(jnp.bfloat16)
            right_rows = lax.dynamic_index_in_dim(masked, second, 1, keepdims=False)
            running = running + jnp.dot(right_rows, amplitude.T, preferred_element_type=jnp.float32)
            return running, None

        running, unused = lax.scan(for_partner, jnp.zeros((NAUX, NVIR), jnp.float32), jnp.arange(OCC, dtype=jnp.int32))
        return running

    gamma = lax.map(for_orbital, jnp.arange(OCC, dtype=jnp.int32))
    return jnp.transpose(gamma, (1, 0, 2)).astype(jnp.bfloat16)
```

```python
import functools

import jax
import jax.numpy as jnp
from jax import lax
from jax.experimental import pallas as pl
from jax.experimental.pallas import tpu as pltpu
from jax.sharding import PartitionSpec as P

MESH = pl.DeviceIdType.MESH
ROWS, NVIR = 320, 896
HALF = NVIR // 2
PIECE = HALF // 4
CUT = 64
WINDOW = 512
JOBS = 5
OWN, NEXT, AFTER, PARTNER = range(4)


def device_at(x, y, z, core):
    return (y * 2 + x % 2, z * 4 + (x // 2) * 2 + core)


def kernel(
    count, pick, occ, vir, b_ref, out,
    rows, flipped, acc, amp, virc, partial, whole, half_whole,
    z1_up, z1_down, z2_up, z2_down, mine, other, back_out, back_in,
    send, recv, b_send, b_recv,
):
    blk, grp = lax.axis_index("blk"), lax.axis_index("grp")
    y, lo = blk // 2, blk % 2
    z, core = grp // 4, grp % 2
    x = ((grp // 2) % 2) * 2 + lo

    sibling = device_at(x, y, z, 1 - core)
    below, above = device_at(x, (y + 3) % 4, z, core), device_at(x, (y + 1) % 4, z, core)
    across = device_at(x, (y + 2) % 4, z, core)
    partner = device_at(x + 1 - 2 * lo, y, z, core)
    far = device_at((x + 2) % 4, y, z, core)
    up, down = device_at(x, y, (z + 1) % 4, core), device_at(x, y, (z + 3) % 4, core)

    own_part = pl.ds(pl.multiple_of(core * ROWS, 16), ROWS)
    started = []

    def start(src, dst, sends, receives, device):
        copy = pltpu.make_async_remote_copy(
            src_ref=src, dst_ref=dst, send_sem=sends, recv_sem=receives,
            device_id=device, device_id_type=MESH,
        )
        copy.start()
        started.append(copy)
        return copy

    line = lax.broadcasted_iota(jnp.int32, (ROWS, NVIR), 0)
    live = jnp.where(line < count[0], b_ref[...].astype(jnp.float32), 0.0).astype(jnp.bfloat16)
    rows[OWN, own_part, :] = live
    half_whole[...] = jnp.zeros_like(half_whole)
    acc[...] = jnp.zeros_like(acc)

    barrier = pltpu.get_barrier_semaphore()
    everyone = (sibling, below, above, across, partner, far, up, down)
    for device in everyone:
        pl.semaphore_signal(barrier, inc=1, device_id=device, device_id_type=MESH)
    pl.semaphore_wait(barrier, len(everyone))

    def spread(slot, index, device):
        return start(
            rows.at[OWN, own_part], rows.at[slot, own_part], b_send.at[index], b_recv.at[index], device
        )

    def pass_on(slot, index):
        return start(
            rows.at[slot, own_part], rows.at[slot, own_part], b_send.at[index], b_recv.at[index], sibling
        )

    own_shared = spread(OWN, 0, sibling)
    next_moved = spread(NEXT, 1, below)
    partner_moved = spread(PARTNER, 2, partner)

    virc[...] = jnp.transpose(jnp.broadcast_to(vir[...], (128, NVIR)))

    def energy(position):
        return occ[pick[position]]

    e_own = energy(blk)
    e_next = energy(((y + 1) % 4) * 2 + lo)
    e_after = energy(((y + 2) % 4) * 2 + lo)
    e_partner = energy(y * 2 + 1 - lo)
    low = lo == 0
    pair_energy = (
        e_own + e_own,
        e_own + e_next,
        e_partner + jnp.where(low, e_own, e_next),
        e_partner + jnp.where(low, e_next, e_after),
        e_own + e_after,
    )
    left = (OWN, OWN, PARTNER, PARTNER, OWN)
    right = (OWN, NEXT, lo, 1 + lo, AFTER)
    turned = y // 2

    def half_rows(which):
        return which * HALF

    def span(which, piece, first=0, size=PIECE):
        return pl.ds(pl.multiple_of(which * HALF + piece * PIECE + first, 16), size)

    def part(piece, first=0, size=PIECE):
        return pl.ds(pl.multiple_of(piece * PIECE + first, 16), size)

    z_up, z_down, z_far = (z + 1) % 4, (z + 3) % 4, (z + 2) % 4

    def window(which):
        flip = (which + turned) % 2
        return pl.ds(pl.multiple_of(flip * (NVIR - WINDOW), 128), WINDOW)

    def width(job):
        return WINDOW if job == 4 else NVIR

    def cols(job):
        return pl.ds(0, width(job))

    def full(job, lines):
        if job == 4:
            return half_whole.at[lines, window(core)]
        return whole.at[job, lines]

    def turn(slot, index):
        def body(step, carry):
            at = pl.ds(pl.multiple_of(step * 128, 128), 128)
            flipped[index, :, at] = jnp.transpose(rows[slot, at, :].astype(jnp.float32)).astype(jnp.bfloat16)
            return carry

        lax.fori_loop(0, 2 * ROWS // 128, body, 0)

    flip_index = (0, 0, 1, 1, 0)
    copies = {}

    def stage0(job):
        lhs = flipped[flip_index[job], pl.ds(pl.multiple_of(core * HALF, 16), HALF), :]
        rhs = rows[right[job], :, window(core)] if job == 4 else rows[right[job]]
        partial[job, :, cols(job)] = jnp.dot(lhs, rhs, preferred_element_type=jnp.float32).astype(jnp.bfloat16)
        copies[job, 0] = start(
            partial.at[job, part(z_far, 0, CUT), cols(job)], z1_up.at[job, :, cols(job)],
            send.at[job, 0], recv.at[job, 0], up,
        )
        copies[job, 1] = start(
            partial.at[job, part(z_far, CUT, PIECE - CUT), cols(job)], z1_down.at[job, :, cols(job)],
            send.at[job, 1], recv.at[job, 1], down,
        )

    def add(job, where, arrived):
        partial[job, where, cols(job)] = (
            partial[job, where, cols(job)].astype(jnp.float32) + arrived[job, :, cols(job)].astype(jnp.float32)
        ).astype(jnp.bfloat16)

    def stage1(job):
        copies[job, 0].wait_recv()
        add(job, part(z_up, 0, CUT), z1_up)
        copies[job, 2] = start(
            partial.at[job, part(z_up), cols(job)], z2_up.at[job, :, cols(job)],
            send.at[job, 2], recv.at[job, 2], up,
        )
        copies[job, 1].wait_recv()
        add(job, part(z_down, CUT, PIECE - CUT), z1_down)
        copies[job, 3] = start(
            partial.at[job, part(z_down), cols(job)], z2_down.at[job, :, cols(job)],
            send.at[job, 3], recv.at[job, 3], down,
        )

    def stage2(job):
        copies[job, 2].wait_recv()
        copies[job, 3].wait_recv()
        w = cols(job)
        mine[job, :, w] = (
            partial[job, part(z), w].astype(jnp.float32)
            + z2_up[job, :, w].astype(jnp.float32)
            + z2_down[job, :, w].astype(jnp.float32)
        ).astype(jnp.bfloat16)
        copies[job, 4] = start(
            mine.at[job, :, w], other.at[job, :, w], send.at[job, 4], recv.at[job, 4], far
        )

    def same(job, lines, index, device):
        copies[job, index] = start(
            full(job, lines), full(job, lines), send.at[job, index], recv.at[job, index], device
        )

    def stage3(job):
        copies[job, 4].wait_recv()
        w = cols(job)
        total = (mine[job, :, w].astype(jnp.float32) + other[job, :, w].astype(jnp.float32)).astype(jnp.bfloat16)
        if job == 4:
            half_whole[span(core, z), window(core)] = total
        else:
            whole[job, span(core, z), :] = total
        same(job, span(core, z), 5, up)
        same(job, span(core, z), 6, down)
        same(job, span(core, z), 7, sibling)

    def stage4(job):
        copies[job, 5].wait_recv()
        same(job, span(core, z_down, 0, CUT), 8, up)
        same(job, span(core, z_down), 9, sibling)
        copies[job, 6].wait_recv()
        same(job, span(core, z_up, CUT, PIECE - CUT), 10, down)
        same(job, span(core, z_up), 11, sibling)

    def stage5(job):
        copies[job, 8].wait_recv()
        copies[job, 10].wait_recv()
        same(job, span(core, z_far), 12, sibling)

    def stage6(job):
        for index in (7, 9, 11, 12):
            copies[job, index].wait_recv()
        source = half_whole if job == 4 else whole.at[job]
        base = pair_energy[job]

        def body(step, carry):
            at = pl.ds(pl.multiple_of(step * 128, 128), 128)
            plain = source[at, :].astype(jnp.float32)
            swapped = jnp.transpose(source[:, at].astype(jnp.float32))
            gap = (base - virc[at, 0:1]) - vir[...]
            value = (2.0 * plain - swapped) / gap
            if job == 4:
                a = lax.broadcasted_iota(jnp.int32, (128, NVIR), 0) + step * 128
                b = lax.broadcasted_iota(jnp.int32, (128, NVIR), 1)
                crossed = (a >= HALF).astype(jnp.int32) + (b >= HALF).astype(jnp.int32)
                value = jnp.where((crossed + turned) % 2 == 0, value, 0.0)
            amp[at, :] = value.astype(jnp.bfloat16)
            return carry

        lax.fori_loop(0, NVIR // 128, body, 0)
        acc[left[job]] = acc[left[job]] + lax.dot_general(
            rows[right[job], own_part, :], amp[...], (((1,), (1,)), ((), ())), preferred_element_type=jnp.float32
        )
        if job > 0:
            acc[right[job]] = acc[right[job]] + jnp.dot(
                rows[left[job], own_part, :], amp[...], preferred_element_type=jnp.float32
            )

    def give_back(slot, index, device):
        back_out[index] = acc[slot].astype(jnp.bfloat16)
        return start(back_out.at[index], back_in.at[index], b_send.at[index + 7], b_recv.at[index + 7], device)

    own_shared.wait_recv()
    turn(OWN, 0)
    stage0(0)
    stage1(0)
    next_moved.wait_recv()
    next_shared = pass_on(NEXT, 3)
    after_moved = spread(AFTER, 4, across)
    stage2(0)
    next_shared.wait_recv()
    stage0(1)
    partner_moved.wait_recv()
    partner_shared = pass_on(PARTNER, 5)
    stage3(0)
    stage1(1)
    partner_shared.wait_recv()
    turn(PARTNER, 1)
    stage0(2)
    stage4(0)
    stage2(1)
    stage1(2)
    after_moved.wait_recv()
    after_shared = pass_on(AFTER, 6)
    stage5(0)
    stage3(1)
    after_shared.wait_recv()
    stage0(3)
    stage2(2)
    stage1(3)
    stage0(4)
    stage6(0)
    stage4(1)
    stage3(2)
    stage2(3)
    stage1(4)
    stage5(1)
    stage4(2)
    stage3(3)
    stage2(4)
    stage6(1)
    stage5(2)
    stage4(3)
    stage3(4)
    stage6(2)
    stage5(3)
    stage4(4)
    stage6(3)
    next_back = give_back(NEXT, 0, above)
    partner_back = give_back(PARTNER, 1, partner)
    stage5(4)
    stage6(4)
    after_back = give_back(AFTER, 2, across)
    next_back.wait_recv()
    partner_back.wait_recv()
    total = acc[OWN] + back_in[0].astype(jnp.float32) + back_in[1].astype(jnp.float32)
    after_back.wait_recv()
    out[...] = (total + back_in[2].astype(jnp.float32)).astype(jnp.bfloat16)
    for copy in started:
        copy.wait_send()


def on_device(b_rows, aux_count, occ_pick, eps_occ, eps_vir):
    bf16, f32 = jnp.bfloat16, jnp.float32
    smem, vmem = pl.BlockSpec(memory_space=pltpu.SMEM), pl.BlockSpec(memory_space=pltpu.VMEM)
    dma = pltpu.SemaphoreType.DMA
    gamma = pl.pallas_call(
        kernel,
        out_shape=jax.ShapeDtypeStruct((ROWS, NVIR), bf16),
        in_specs=[smem, smem, smem, vmem, vmem],
        out_specs=vmem,
        scratch_shapes=[
            pltpu.VMEM((4, 2 * ROWS, NVIR), bf16),
            pltpu.VMEM((2, NVIR, 2 * ROWS), bf16),
            pltpu.VMEM((4, ROWS, NVIR), f32),
            pltpu.VMEM((NVIR, NVIR), bf16),
            pltpu.VMEM((NVIR, 128), f32),
            pltpu.VMEM((JOBS, HALF, NVIR), bf16),
            pltpu.VMEM((JOBS - 1, NVIR, NVIR), bf16),
            pltpu.VMEM((NVIR, NVIR), bf16),
            pltpu.VMEM((JOBS, CUT, NVIR), bf16),
            pltpu.VMEM((JOBS, PIECE - CUT, NVIR), bf16),
            pltpu.VMEM((JOBS, PIECE, NVIR), bf16),
            pltpu.VMEM((JOBS, PIECE, NVIR), bf16),
            pltpu.VMEM((JOBS, PIECE, NVIR), bf16),
            pltpu.VMEM((JOBS, PIECE, NVIR), bf16),
            pltpu.VMEM((3, ROWS, NVIR), bf16),
            pltpu.VMEM((3, ROWS, NVIR), bf16),
            dma((JOBS, 13)), dma((JOBS, 13)), dma((10,)), dma((10,)),
        ],
        compiler_params=pltpu.CompilerParams(
            collective_id=0, has_side_effects=True, vmem_limit_bytes=56 * 2**20
        ),
    )(aux_count, occ_pick, eps_occ, eps_vir.reshape(1, NVIR), b_rows[:, 0, :])
    return gamma[:, None, :]


def solution(mesh):
    placed = (P("grp", "blk", None), P("grp"), P(), P(), P())
    return jax.shard_map(
        on_device, mesh=mesh, in_specs=placed, out_specs=P("grp", "blk", None), check_vma=False
    )
```

```python
import jax
import jax.numpy as jnp
from jax import lax
from jax.experimental import pallas as pl
from jax.experimental.pallas import tpu as pltpu
from jax.sharding import PartitionSpec as P

MESH = pl.DeviceIdType.MESH
ROWS, NVIR = 320, 896
HALF = NVIR // 2
PIECE = HALF // 4
CUT = 64
SPLIT = 512
WINDOW = 512
OWN, NEXT, PREV, MATE = range(4)
JOBS = 5
CHUNKS = ((0, 0, 896), (1, 0, 896), (2, 0, 896), (3, 0, 896), (4, 0, 512))


def device_at(x, y, z, core):
    return (y * 2 + x % 2, z * 4 + (x // 2) * 2 + core)


def kernel(
    count, pick, occ, vir, b_ref, out,
    rows, flipped, acc, amp, virc, partial, whole, half_whole,
    z1_up, z1_down, z2_up, z2_down, mine, other, back_out, back_in,
    send, recv, b_send, b_recv,
):
    blk, grp = lax.axis_index("blk"), lax.axis_index("grp")
    y, lo = blk // 2, blk % 2
    z, core = grp // 4, grp % 2
    x = ((grp // 2) % 2) * 2 + lo
    y_up, y_down = (y + 1) % 4, (y + 3) % 4

    sibling = device_at(x, y, z, 1 - core)
    above, below = device_at(x, y_up, z, core), device_at(x, y_down, z, core)
    partner = device_at(x + 1 - 2 * lo, y, z, core)
    diagonal = device_at(x + 1 - 2 * lo, (y + 3 + 2 * lo) % 4, z, core)
    giver = device_at(x + 1 - 2 * lo, (y + lo) % 4, z, core)
    far = device_at((x + 2) % 4, y, z, core)
    up, down = device_at(x, y, (z + 1) % 4, core), device_at(x, y, (z + 3) % 4, core)

    own_part = pl.ds(pl.multiple_of(core * ROWS, 16), ROWS)
    started = []

    def remote(src, dst, sends, receives, device):
        copy = pltpu.make_async_remote_copy(
            src_ref=src, dst_ref=dst, send_sem=sends, recv_sem=receives,
            device_id=device, device_id_type=MESH,
        )
        started.append(copy)
        return copy

    def start(*where):
        copy = remote(*where)
        copy.start()
        return copy

    line = lax.broadcasted_iota(jnp.int32, (ROWS, NVIR), 0)
    live = jnp.where(line < count[0], b_ref[...].astype(jnp.float32), 0.0).astype(jnp.bfloat16)
    rows[OWN, own_part, :] = live
    half_whole[...] = jnp.zeros_like(half_whole)

    barrier = pltpu.get_barrier_semaphore()
    everyone = (sibling, above, below, partner, diagonal, far, up, down)
    for device in everyone:
        pl.semaphore_signal(barrier, inc=1, device_id=device, device_id_type=MESH)
    pl.semaphore_wait(barrier, len(everyone))

    first, second = pl.ds(0, SPLIT), pl.ds(SPLIT, NVIR - SPLIT)
    everything = pl.ds(0, NVIR)

    def spread(slot, columns, index, device):
        return start(
            rows.at[OWN, own_part, columns], rows.at[slot, own_part, columns],
            b_send.at[index], b_recv.at[index], device,
        )

    def pass_on(slot, columns, index):
        return start(
            rows.at[slot, own_part, columns], rows.at[slot, own_part, columns],
            b_send.at[index], b_recv.at[index], sibling,
        )

    def to_partner(columns, index):
        return remote(
            rows.at[(1 - lo) * NEXT, own_part, columns], rows.at[MATE, own_part, columns],
            b_send.at[index], b_recv.at[index], partner,
        )

    copies = {}
    copies["own"] = spread(OWN, everything, 0, sibling)
    copies["next a"] = spread(NEXT, first, 1, below)
    copies["next b"] = spread(NEXT, second, 2, below)
    copies["prev"] = spread(PREV, everything, 3, above)
    copies["mate a"] = to_partner(first, 4)
    copies["mate b"] = to_partner(second, 5)

    @pl.when(lo == 1)
    def _():
        copies["mate a"].start()
        copies["mate b"].start()

    acc[...] = jnp.zeros_like(acc)
    virc[...] = jnp.transpose(jnp.broadcast_to(vir[...], (128, NVIR)))

    def energy(position):
        return occ[pick[position]]

    e_own = energy(blk)
    e_next = energy(y_up * 2 + lo)
    e_prev = energy(y_down * 2 + lo)
    e_mate = energy(((y + lo) % 4) * 2 + 1 - lo)
    pair_energy = (e_own + e_own, e_own + e_next, e_mate + e_own, e_mate + e_prev, e_prev + e_next)
    left = (OWN, OWN, MATE, MATE, PREV)
    right = (OWN, NEXT, OWN, PREV, NEXT)
    turned = y // 2

    def span(which, piece, first=0, size=PIECE):
        return pl.ds(pl.multiple_of(which * HALF + piece * PIECE + first, 16), size)

    def part(piece, first=0, size=PIECE):
        return pl.ds(pl.multiple_of(piece * PIECE + first, 16), size)

    z_up, z_down, z_far = (z + 1) % 4, (z + 3) % 4, (z + 2) % 4
    flip = (core + turned) % 2
    window = pl.ds(pl.multiple_of(flip * (NVIR - WINDOW), 128), WINDOW)

    def at(chunk):
        job, begin, size = CHUNKS[chunk]
        return job, pl.ds(begin, size)

    def full(chunk, lines):
        job, w = at(chunk)
        if job == 4:
            return half_whole.at[lines, window]
        return whole.at[job, lines, w]

    def turn(slot, index):
        def body(step, carry):
            lines = pl.ds(pl.multiple_of(step * 128, 128), 128)
            flipped[index, :, lines] = jnp.transpose(rows[slot, lines, :].astype(jnp.float32)).astype(jnp.bfloat16)
            return carry

        lax.fori_loop(0, 2 * ROWS // 128, body, 0)

    flip_index = (0, 0, 1, 1, 2)
    arrived = set()

    def need(*names):
        for name in names:
            if name not in arrived:
                arrived.add(name)
                copies[name].wait_recv()

    def own():
        copies["own"].wait_recv()
        turn(OWN, 0)

    def next_a():
        copies["next a"].wait_recv()
        copies["next a on"] = pass_on(NEXT, first, 6)
        pl.when(lo == 0)(copies["mate a"].start)

    def next_b():
        copies["next b"].wait_recv()
        copies["next b on"] = pass_on(NEXT, second, 7)
        pl.when(lo == 0)(copies["mate b"].start)

    def prev():
        copies["prev"].wait_recv()
        copies["prev on"] = pass_on(PREV, everything, 8)

    def turn_prev():
        need("prev on")
        turn(PREV, 2)

    def mate():
        copies["mate a"].wait_recv()
        copies["mate b"].wait_recv()
        copies["mate on"] = pass_on(MATE, everything, 9)

    def turn_mate():
        copies["mate on"].wait_recv()
        turn(MATE, 1)

    def stage0(chunk):
        job, w = at(chunk)
        if job in (1, 4):
            need("next a on")
            if job == 4 or w.start + w.size > SPLIT:
                need("next b on")
        if job == 3:
            need("prev on")
        lhs = flipped[flip_index[job], pl.ds(pl.multiple_of(core * HALF, 16), HALF), :]
        rhs = rows[right[job], :, window] if job == 4 else rows[right[job], :, w]
        partial[job, :, w] = jnp.dot(lhs, rhs, preferred_element_type=jnp.float32).astype(jnp.bfloat16)
        copies[chunk, 0] = start(
            partial.at[job, part(z_far, 0, CUT), w], z1_up.at[job, :, w],
            send.at[chunk, 0], recv.at[chunk, 0], up,
        )
        copies[chunk, 1] = start(
            partial.at[job, part(z_far, CUT, PIECE - CUT), w], z1_down.at[job, :, w],
            send.at[chunk, 1], recv.at[chunk, 1], down,
        )

    def add(job, w, where, arrived):
        partial[job, where, w] = (
            partial[job, where, w].astype(jnp.float32) + arrived[job, :, w].astype(jnp.float32)
        ).astype(jnp.bfloat16)

    def stage1(chunk):
        job, w = at(chunk)
        copies[chunk, 0].wait_recv()
        add(job, w, part(z_up, 0, CUT), z1_up)
        copies[chunk, 2] = start(
            partial.at[job, part(z_up), w], z2_up.at[job, :, w], send.at[chunk, 2], recv.at[chunk, 2], up
        )
        copies[chunk, 1].wait_recv()
        add(job, w, part(z_down, CUT, PIECE - CUT), z1_down)
        copies[chunk, 3] = start(
            partial.at[job, part(z_down), w], z2_down.at[job, :, w], send.at[chunk, 3], recv.at[chunk, 3], down
        )

    def stage2(chunk):
        job, w = at(chunk)
        copies[chunk, 2].wait_recv()
        copies[chunk, 3].wait_recv()
        mine[job, :, w] = (
            partial[job, part(z), w].astype(jnp.float32)
            + z2_up[job, :, w].astype(jnp.float32)
            + z2_down[job, :, w].astype(jnp.float32)
        ).astype(jnp.bfloat16)
        copies[chunk, 4] = start(
            mine.at[job, :, w], other.at[job, :, w], send.at[chunk, 4], recv.at[chunk, 4], far
        )

    def same(chunk, lines, index, device):
        copies[chunk, index] = start(
            full(chunk, lines), full(chunk, lines), send.at[chunk, index], recv.at[chunk, index], device
        )

    def stage3(chunk):
        job, w = at(chunk)
        copies[chunk, 4].wait_recv()
        total = (mine[job, :, w].astype(jnp.float32) + other[job, :, w].astype(jnp.float32)).astype(jnp.bfloat16)
        if job == 4:
            half_whole[span(core, z), window] = total
        else:
            whole[job, span(core, z), w] = total
        same(chunk, span(core, z), 5, up)
        same(chunk, span(core, z), 6, down)
        same(chunk, span(core, z), 7, sibling)

    def stage4(chunk):
        copies[chunk, 5].wait_recv()
        same(chunk, span(core, z_down, 0, CUT), 8, up)
        same(chunk, span(core, z_down), 9, sibling)
        copies[chunk, 6].wait_recv()
        same(chunk, span(core, z_up, CUT, PIECE - CUT), 10, down)
        same(chunk, span(core, z_up), 11, sibling)

    def stage5(chunk):
        copies[chunk, 8].wait_recv()
        copies[chunk, 10].wait_recv()
        same(chunk, span(core, z_far), 12, sibling)

    def stage6(job):
        for chunk in range(len(CHUNKS)):
            if CHUNKS[chunk][0] == job:
                for index in (7, 9, 11, 12):
                    copies[chunk, index].wait_recv()
        source = half_whole if job == 4 else whole.at[job]
        base = pair_energy[job]

        def body(step, carry):
            lines = pl.ds(pl.multiple_of(step * 128, 128), 128)
            plain = source[lines, :].astype(jnp.float32)
            swapped = jnp.transpose(source[:, lines].astype(jnp.float32))
            gap = (base - virc[lines, 0:1]) - vir[...]
            value = (2.0 * plain - swapped) / gap
            if job == 4:
                a = lax.broadcasted_iota(jnp.int32, (128, NVIR), 0) + step * 128
                b = lax.broadcasted_iota(jnp.int32, (128, NVIR), 1)
                crossed = (a >= HALF).astype(jnp.int32) + (b >= HALF).astype(jnp.int32)
                value = jnp.where((crossed + turned) % 2 == 0, value, 0.0)
            amp[lines, :] = value.astype(jnp.bfloat16)
            return carry

        lax.fori_loop(0, NVIR // 128, body, 0)
        acc[left[job]] = acc[left[job]] + lax.dot_general(
            rows[right[job], own_part, :], amp[...], (((1,), (1,)), ((), ())), preferred_element_type=jnp.float32
        )
        if job > 0:
            acc[right[job]] = acc[right[job]] + jnp.dot(
                rows[left[job], own_part, :], amp[...], preferred_element_type=jnp.float32
            )

    def give_back(slot, device):
        index = slot - 1
        back_out[index] = acc[slot].astype(jnp.bfloat16)
        copies[slot] = start(
            back_out.at[index], back_in.at[index], b_send.at[10 + index], b_recv.at[10 + index], device
        )

    own()
    stage0(0)
    stage1(0)
    next_a()
    next_b()
    prev()
    stage0(1)
    turn_prev()
    stage0(4)
    stage1(1)
    stage1(4)
    mate()
    turn_mate()
    stage0(3)
    stage2(0)
    stage0(2)
    stage2(1)
    stage1(3)
    stage2(4)
    stage1(2)
    stage2(3)
    stage3(1)
    stage3(4)
    stage2(2)
    stage4(1)
    stage4(4)
    stage3(3)
    stage5(1)
    stage3(2)
    stage5(4)
    stage6(1)
    stage4(3)
    stage6(4)
    give_back(NEXT, above)
    stage4(2)
    stage3(0)
    stage5(3)
    stage5(2)
    stage6(3)
    stage6(2)
    give_back(MATE, giver)
    stage4(0)
    give_back(PREV, below)
    stage5(0)
    stage6(0)
    for slot in (NEXT, PREV, MATE):
        copies[slot].wait_recv()
    total = acc[OWN] + back_in[0].astype(jnp.float32)
    total = total + back_in[1].astype(jnp.float32) + back_in[2].astype(jnp.float32)
    out[...] = total.astype(jnp.bfloat16)
    for copy in started:
        copy.wait_send()


def on_device(b_rows, aux_count, occ_pick, eps_occ, eps_vir):
    bf16, f32 = jnp.bfloat16, jnp.float32
    smem, vmem = pl.BlockSpec(memory_space=pltpu.SMEM), pl.BlockSpec(memory_space=pltpu.VMEM)
    dma = pltpu.SemaphoreType.DMA
    gamma = pl.pallas_call(
        kernel,
        out_shape=jax.ShapeDtypeStruct((ROWS, NVIR), bf16),
        in_specs=[smem, smem, smem, vmem, vmem],
        out_specs=vmem,
        scratch_shapes=[
            pltpu.VMEM((4, 2 * ROWS, NVIR), bf16),
            pltpu.VMEM((3, NVIR, 2 * ROWS), bf16),
            pltpu.VMEM((4, ROWS, NVIR), f32),
            pltpu.VMEM((NVIR, NVIR), bf16),
            pltpu.VMEM((NVIR, 128), f32),
            pltpu.VMEM((JOBS, HALF, NVIR), bf16),
            pltpu.VMEM((JOBS - 1, NVIR, NVIR), bf16),
            pltpu.VMEM((NVIR, NVIR), bf16),
            pltpu.VMEM((JOBS, CUT, NVIR), bf16),
            pltpu.VMEM((JOBS, PIECE - CUT, NVIR), bf16),
            pltpu.VMEM((JOBS, PIECE, NVIR), bf16),
            pltpu.VMEM((JOBS, PIECE, NVIR), bf16),
            pltpu.VMEM((JOBS, PIECE, NVIR), bf16),
            pltpu.VMEM((JOBS, PIECE, NVIR), bf16),
            pltpu.VMEM((3, ROWS, NVIR), bf16),
            pltpu.VMEM((3, ROWS, NVIR), bf16),
            dma((len(CHUNKS), 13)), dma((len(CHUNKS), 13)), dma((13,)), dma((13,)),
        ],
        compiler_params=pltpu.CompilerParams(
            collective_id=0, has_side_effects=True, vmem_limit_bytes=56 * 2**20
        ),
    )(aux_count, occ_pick, eps_occ, eps_vir.reshape(1, NVIR), b_rows[:, 0, :])
    return gamma[:, None, :]


def solution(mesh):
    placed = (P("grp", "blk", None), P("grp"), P(), P(), P())
    return jax.shard_map(
        on_device, mesh=mesh, in_specs=placed, out_specs=P("grp", "blk", None), check_vma=False
    )
```

```python
import jax
import jax.numpy as jnp
from jax import lax
from jax.experimental import pallas as pl
from jax.experimental.pallas import tpu as pltpu
from jax.sharding import PartitionSpec as P

MESH = pl.DeviceIdType.MESH
ROWS, NVIR = 320, 896
HALF = NVIR // 2
PIECE = HALF // 4
CUT = 64
SPLIT = 512
WINDOW = 512
OWN, NEXT, PREV, MATE = range(4)
JOBS = 5
CHUNKS = ((0, 0, 512), (0, 512, 384), (1, 0, 512), (1, 512, 384), (2, 0, 512), (2, 512, 384), (3, 0, 512), (3, 512, 384), (4, 0, 512))


def device_at(x, y, z, core):
    return (y * 2 + x % 2, z * 4 + (x // 2) * 2 + core)


def kernel(
    count, pick, occ, vir, b_ref, out,
    rows, flipped, acc, amp, virc, partial, whole, half_whole,
    z1_up, z1_down, z2_up, z2_down, mine, other, back_out, back_in,
    send, recv, b_send, b_recv,
):
    blk, grp = lax.axis_index("blk"), lax.axis_index("grp")
    y, lo = blk // 2, blk % 2
    z, core = grp // 4, grp % 2
    x = ((grp // 2) % 2) * 2 + lo
    y_up, y_down = (y + 1) % 4, (y + 3) % 4

    sibling = device_at(x, y, z, 1 - core)
    above, below = device_at(x, y_up, z, core), device_at(x, y_down, z, core)
    partner = device_at(x + 1 - 2 * lo, y, z, core)
    diagonal = device_at(x + 1 - 2 * lo, (y + 3 + 2 * lo) % 4, z, core)
    giver = device_at(x + 1 - 2 * lo, (y + lo) % 4, z, core)
    far = device_at((x + 2) % 4, y, z, core)
    up, down = device_at(x, y, (z + 1) % 4, core), device_at(x, y, (z + 3) % 4, core)

    own_part = pl.ds(pl.multiple_of(core * ROWS, 16), ROWS)
    started = []

    def remote(src, dst, sends, receives, device):
        copy = pltpu.make_async_remote_copy(
            src_ref=src, dst_ref=dst, send_sem=sends, recv_sem=receives,
            device_id=device, device_id_type=MESH,
        )
        started.append(copy)
        return copy

    def start(*where):
        copy = remote(*where)
        copy.start()
        return copy

    line = lax.broadcasted_iota(jnp.int32, (ROWS, NVIR), 0)
    live = jnp.where(line < count[0], b_ref[...].astype(jnp.float32), 0.0).astype(jnp.bfloat16)
    rows[OWN, own_part, :] = live
    half_whole[...] = jnp.zeros_like(half_whole)

    barrier = pltpu.get_barrier_semaphore()
    everyone = (sibling, above, below, partner, diagonal, far, up, down)
    for device in everyone:
        pl.semaphore_signal(barrier, inc=1, device_id=device, device_id_type=MESH)
    pl.semaphore_wait(barrier, len(everyone))

    first, second = pl.ds(0, SPLIT), pl.ds(SPLIT, NVIR - SPLIT)
    everything = pl.ds(0, NVIR)

    def spread(slot, columns, index, device):
        return start(
            rows.at[OWN, own_part, columns], rows.at[slot, own_part, columns],
            b_send.at[index], b_recv.at[index], device,
        )

    def pass_on(slot, columns, index):
        return start(
            rows.at[slot, own_part, columns], rows.at[slot, own_part, columns],
            b_send.at[index], b_recv.at[index], sibling,
        )

    def to_partner(columns, index):
        return remote(
            rows.at[(1 - lo) * NEXT, own_part, columns], rows.at[MATE, own_part, columns],
            b_send.at[index], b_recv.at[index], partner,
        )

    copies = {}
    copies["own"] = spread(OWN, everything, 0, sibling)
    copies["next a"] = spread(NEXT, first, 1, below)
    copies["next b"] = spread(NEXT, second, 2, below)
    copies["prev"] = spread(PREV, everything, 3, above)
    copies["mate a"] = to_partner(first, 4)
    copies["mate b"] = to_partner(second, 5)

    @pl.when(lo == 1)
    def _():
        copies["mate a"].start()
        copies["mate b"].start()

    acc[...] = jnp.zeros_like(acc)
    virc[...] = jnp.transpose(jnp.broadcast_to(vir[...], (128, NVIR)))

    def energy(position):
        return occ[pick[position]]

    e_own = energy(blk)
    e_next = energy(y_up * 2 + lo)
    e_prev = energy(y_down * 2 + lo)
    e_mate = energy(((y + lo) % 4) * 2 + 1 - lo)
    pair_energy = (e_own + e_own, e_own + e_next, e_mate + e_own, e_mate + e_prev, e_prev + e_next)
    left = (OWN, OWN, MATE, MATE, PREV)
    right = (OWN, NEXT, OWN, PREV, NEXT)
    turned = y // 2

    def span(which, piece, first=0, size=PIECE):
        return pl.ds(pl.multiple_of(which * HALF + piece * PIECE + first, 16), size)

    def part(piece, first=0, size=PIECE):
        return pl.ds(pl.multiple_of(piece * PIECE + first, 16), size)

    z_up, z_down, z_far = (z + 1) % 4, (z + 3) % 4, (z + 2) % 4
    flip = (core + turned) % 2
    window = pl.ds(pl.multiple_of(flip * (NVIR - WINDOW), 128), WINDOW)

    def at(chunk):
        job, begin, size = CHUNKS[chunk]
        return job, pl.ds(begin, size)

    def full(chunk, lines):
        job, w = at(chunk)
        if job == 4:
            return half_whole.at[lines, window]
        return whole.at[job, lines, w]

    def turn(slot, index):
        def body(step, carry):
            lines = pl.ds(pl.multiple_of(step * 128, 128), 128)
            flipped[index, :, lines] = jnp.transpose(rows[slot, lines, :].astype(jnp.float32)).astype(jnp.bfloat16)
            return carry

        lax.fori_loop(0, 2 * ROWS // 128, body, 0)

    flip_index = (0, 0, 1, 1, 2)
    arrived = set()

    def need(*names):
        for name in names:
            if name not in arrived:
                arrived.add(name)
                copies[name].wait_recv()

    def own():
        copies["own"].wait_recv()
        turn(OWN, 0)

    def next_a():
        copies["next a"].wait_recv()
        copies["next a on"] = pass_on(NEXT, first, 6)
        pl.when(lo == 0)(copies["mate a"].start)

    def next_b():
        copies["next b"].wait_recv()
        copies["next b on"] = pass_on(NEXT, second, 7)
        pl.when(lo == 0)(copies["mate b"].start)

    def prev():
        copies["prev"].wait_recv()
        copies["prev on"] = pass_on(PREV, everything, 8)

    def turn_prev():
        need("prev on")
        turn(PREV, 2)

    def mate():
        copies["mate a"].wait_recv()
        copies["mate b"].wait_recv()
        copies["mate on"] = pass_on(MATE, everything, 9)

    def turn_mate():
        copies["mate on"].wait_recv()
        turn(MATE, 1)

    def stage0(chunk):
        job, w = at(chunk)
        if job in (1, 4):
            need("next a on")
            if job == 4 or w.start + w.size > SPLIT:
                need("next b on")
        if job == 3:
            need("prev on")
        lhs = flipped[flip_index[job], pl.ds(pl.multiple_of(core * HALF, 16), HALF), :]
        rhs = rows[right[job], :, window] if job == 4 else rows[right[job], :, w]
        partial[job, :, w] = jnp.dot(lhs, rhs, preferred_element_type=jnp.float32).astype(jnp.bfloat16)
        copies[chunk, 0] = start(
            partial.at[job, part(z_far, 0, CUT), w], z1_up.at[job, :, w],
            send.at[chunk, 0], recv.at[chunk, 0], up,
        )
        copies[chunk, 1] = start(
            partial.at[job, part(z_far, CUT, PIECE - CUT), w], z1_down.at[job, :, w],
            send.at[chunk, 1], recv.at[chunk, 1], down,
        )

    def add(job, w, where, arrived):
        partial[job, where, w] = (
            partial[job, where, w].astype(jnp.float32) + arrived[job, :, w].astype(jnp.float32)
        ).astype(jnp.bfloat16)

    def stage1(chunk):
        job, w = at(chunk)
        copies[chunk, 0].wait_recv()
        add(job, w, part(z_up, 0, CUT), z1_up)
        copies[chunk, 2] = start(
            partial.at[job, part(z_up), w], z2_up.at[job, :, w], send.at[chunk, 2], recv.at[chunk, 2], up
        )
        copies[chunk, 1].wait_recv()
        add(job, w, part(z_down, CUT, PIECE - CUT), z1_down)
        copies[chunk, 3] = start(
            partial.at[job, part(z_down), w], z2_down.at[job, :, w], send.at[chunk, 3], recv.at[chunk, 3], down
        )

    def stage2(chunk):
        job, w = at(chunk)
        copies[chunk, 2].wait_recv()
        copies[chunk, 3].wait_recv()
        mine[job, :, w] = (
            partial[job, part(z), w].astype(jnp.float32)
            + z2_up[job, :, w].astype(jnp.float32)
            + z2_down[job, :, w].astype(jnp.float32)
        ).astype(jnp.bfloat16)
        copies[chunk, 4] = start(
            mine.at[job, :, w], other.at[job, :, w], send.at[chunk, 4], recv.at[chunk, 4], far
        )

    def same(chunk, lines, index, device):
        copies[chunk, index] = start(
            full(chunk, lines), full(chunk, lines), send.at[chunk, index], recv.at[chunk, index], device
        )

    def stage3(chunk):
        job, w = at(chunk)
        copies[chunk, 4].wait_recv()
        total = (mine[job, :, w].astype(jnp.float32) + other[job, :, w].astype(jnp.float32)).astype(jnp.bfloat16)
        if job == 4:
            half_whole[span(core, z), window] = total
        else:
            whole[job, span(core, z), w] = total
        same(chunk, span(core, z), 5, up)
        same(chunk, span(core, z), 6, down)
        same(chunk, span(core, z), 7, sibling)

    def stage4(chunk):
        copies[chunk, 5].wait_recv()
        same(chunk, span(core, z_down, 0, CUT), 8, up)
        same(chunk, span(core, z_down), 9, sibling)
        copies[chunk, 6].wait_recv()
        same(chunk, span(core, z_up, CUT, PIECE - CUT), 10, down)
        same(chunk, span(core, z_up), 11, sibling)

    def stage5(chunk):
        copies[chunk, 8].wait_recv()
        copies[chunk, 10].wait_recv()
        same(chunk, span(core, z_far), 12, sibling)

    def stage6(job):
        for chunk in range(len(CHUNKS)):
            if CHUNKS[chunk][0] == job:
                for index in (7, 9, 11, 12):
                    copies[chunk, index].wait_recv()
        source = half_whole if job == 4 else whole.at[job]
        base = pair_energy[job]

        def body(step, carry):
            lines = pl.ds(pl.multiple_of(step * 128, 128), 128)
            plain = source[lines, :].astype(jnp.float32)
            swapped = jnp.transpose(source[:, lines].astype(jnp.float32))
            gap = (base - virc[lines, 0:1]) - vir[...]
            value = (2.0 * plain - swapped) / gap
            if job == 4:
                a = lax.broadcasted_iota(jnp.int32, (128, NVIR), 0) + step * 128
                b = lax.broadcasted_iota(jnp.int32, (128, NVIR), 1)
                crossed = (a >= HALF).astype(jnp.int32) + (b >= HALF).astype(jnp.int32)
                value = jnp.where((crossed + turned) % 2 == 0, value, 0.0)
            amp[lines, :] = value.astype(jnp.bfloat16)
            return carry

        lax.fori_loop(0, NVIR // 128, body, 0)
        acc[left[job]] = acc[left[job]] + lax.dot_general(
            rows[right[job], own_part, :], amp[...], (((1,), (1,)), ((), ())), preferred_element_type=jnp.float32
        )
        if job > 0:
            acc[right[job]] = acc[right[job]] + jnp.dot(
                rows[left[job], own_part, :], amp[...], preferred_element_type=jnp.float32
            )

    def give_back(slot, device):
        index = slot - 1
        back_out[index] = acc[slot].astype(jnp.bfloat16)
        copies[slot] = start(
            back_out.at[index], back_in.at[index], b_send.at[10 + index], b_recv.at[10 + index], device
        )

    own()
    stage0(0)
    stage1(0)
    next_a()
    stage0(1)
    stage0(2)
    stage1(1)
    next_b()
    stage1(2)
    prev()
    stage0(3)
    turn_prev()
    stage0(8)
    stage2(2)
    stage1(3)
    stage1(8)
    mate()
    stage3(2)
    turn_mate()
    stage0(4)
    stage2(3)
    stage0(6)
    stage2(8)
    stage0(5)
    stage4(2)
    stage0(7)
    stage1(5)
    stage1(4)
    stage3(8)
    stage3(3)
    stage2(4)
    stage1(6)
    stage2(5)
    stage4(3)
    stage4(8)
    stage1(7)
    stage2(6)
    stage3(5)
    stage5(2)
    stage5(3)
    stage3(4)
    stage5(8)
    stage2(0)
    stage6(1)
    stage2(7)
    stage4(5)
    stage3(6)
    stage6(4)
    stage4(4)
    stage3(7)
    give_back(NEXT, above)
    stage2(1)
    stage5(5)
    stage5(4)
    stage4(6)
    stage4(7)
    stage6(2)
    stage5(6)
    stage5(7)
    stage3(1)
    stage6(3)
    give_back(MATE, giver)
    give_back(PREV, below)
    stage3(0)
    stage4(1)
    stage5(1)
    stage4(0)
    stage5(0)
    stage6(0)
    for slot in (NEXT, PREV, MATE):
        copies[slot].wait_recv()
    total = acc[OWN] + back_in[0].astype(jnp.float32)
    total = total + back_in[1].astype(jnp.float32) + back_in[2].astype(jnp.float32)
    out[...] = total.astype(jnp.bfloat16)
    for copy in started:
        copy.wait_send()


def on_device(b_rows, aux_count, occ_pick, eps_occ, eps_vir):
    bf16, f32 = jnp.bfloat16, jnp.float32
    smem, vmem = pl.BlockSpec(memory_space=pltpu.SMEM), pl.BlockSpec(memory_space=pltpu.VMEM)
    dma = pltpu.SemaphoreType.DMA
    gamma = pl.pallas_call(
        kernel,
        out_shape=jax.ShapeDtypeStruct((ROWS, NVIR), bf16),
        in_specs=[smem, smem, smem, vmem, vmem],
        out_specs=vmem,
        scratch_shapes=[
            pltpu.VMEM((4, 2 * ROWS, NVIR), bf16),
            pltpu.VMEM((3, NVIR, 2 * ROWS), bf16),
            pltpu.VMEM((4, ROWS, NVIR), f32),
            pltpu.VMEM((NVIR, NVIR), bf16),
            pltpu.VMEM((NVIR, 128), f32),
            pltpu.VMEM((JOBS, HALF, NVIR), bf16),
            pltpu.VMEM((JOBS - 1, NVIR, NVIR), bf16),
            pltpu.VMEM((NVIR, NVIR), bf16),
            pltpu.VMEM((JOBS, CUT, NVIR), bf16),
            pltpu.VMEM((JOBS, PIECE - CUT, NVIR), bf16),
            pltpu.VMEM((JOBS, PIECE, NVIR), bf16),
            pltpu.VMEM((JOBS, PIECE, NVIR), bf16),
            pltpu.VMEM((JOBS, PIECE, NVIR), bf16),
            pltpu.VMEM((JOBS, PIECE, NVIR), bf16),
            pltpu.VMEM((3, ROWS, NVIR), bf16),
            pltpu.VMEM((3, ROWS, NVIR), bf16),
            dma((len(CHUNKS), 13)), dma((len(CHUNKS), 13)), dma((13,)), dma((13,)),
        ],
        compiler_params=pltpu.CompilerParams(
            collective_id=0, has_side_effects=True, vmem_limit_bytes=56 * 2**20
        ),
    )(aux_count, occ_pick, eps_occ, eps_vir.reshape(1, NVIR), b_rows[:, 0, :])
    return gamma[:, None, :]


def solution(mesh):
    placed = (P("grp", "blk", None), P("grp"), P(), P(), P())
    return jax.shard_map(
        on_device, mesh=mesh, in_specs=placed, out_specs=P("grp", "blk", None), check_vma=False
    )
```

```python
import jax
import jax.numpy as jnp
from jax import lax
from jax.experimental import pallas as pl
from jax.experimental.pallas import tpu as pltpu
from jax.sharding import PartitionSpec as P

MESH = pl.DeviceIdType.MESH
ROWS, NVIR = 320, 896
HALF = NVIR // 2
PIECE = HALF // 4
CUTS = (64, 48)
SPLIT = 512
WINDOW = 512
OWN, NEXT, PREV, MATE = range(4)
JOBS = 5
CHUNKS = ((0, 0, 512), (0, 512, 384), (1, 0, 512), (1, 512, 384), (2, 0, 512), (2, 512, 384), (3, 0, 512), (3, 512, 384), (4, 0, 512))
TURNS = (1, 0, 0, 1, 1, 0, 1, 0, 0)


def device_at(x, y, z, core):
    return (y * 2 + x % 2, z * 4 + (x // 2) * 2 + core)


def kernel(
    count_ref, pick_ref, occ_ref, vir, b_ref, out,
    count, pick, occ, small,
    rows, flipped, acc, amp, virc, virr, partial, whole, half_whole,
    z1_up, z1_down, z2_up, z2_down, mine, other, back_out, back_in,
    send, recv, b_send, b_recv,
):
    blk, grp = lax.axis_index("blk"), lax.axis_index("grp")
    y, lo = blk // 2, blk % 2
    z, core = grp // 4, grp % 2
    x = ((grp // 2) % 2) * 2 + lo
    y_up, y_down = (y + 1) % 4, (y + 3) % 4

    sibling = device_at(x, y, z, 1 - core)
    above, below = device_at(x, y_up, z, core), device_at(x, y_down, z, core)
    partner = device_at(x + 1 - 2 * lo, y, z, core)
    diagonal = device_at(x + 1 - 2 * lo, (y + 3 + 2 * lo) % 4, z, core)
    giver = device_at(x + 1 - 2 * lo, (y + lo) % 4, z, core)
    far = device_at((x + 2) % 4, y, z, core)
    up, down = device_at(x, y, (z + 1) % 4, core), device_at(x, y, (z + 3) % 4, core)

    own_part = pl.ds(pl.multiple_of(core * ROWS, 16), ROWS)
    started = []

    def remote(src, dst, sends, receives, device):
        copy = pltpu.make_async_remote_copy(
            src_ref=src, dst_ref=dst, send_sem=sends, recv_sem=receives,
            device_id=device, device_id_type=MESH,
        )
        started.append(copy)
        return copy

    def start(*where):
        copy = remote(*where)
        copy.start()
        return copy

    fetches = [
        pltpu.make_async_copy(src, dst, small.at[index])
        for index, (src, dst) in enumerate(
            ((b_ref, rows.at[OWN, own_part]), (count_ref, count), (pick_ref, pick), (occ_ref, occ))
        )
    ]
    for fetch in fetches:
        fetch.start()
    half_whole[...] = jnp.zeros_like(half_whole)

    barrier = pltpu.get_barrier_semaphore()
    everyone = (sibling, above, below, partner, diagonal, far, up, down)
    for device in everyone:
        pl.semaphore_signal(barrier, inc=1, device_id=device, device_id_type=MESH)

    acc[...] = jnp.zeros_like(acc)
    virc[...] = jnp.transpose(jnp.broadcast_to(vir[...].reshape(1, NVIR), (128, NVIR)))
    virr[...] = jnp.broadcast_to(vir[...].reshape(1, NVIR), (8, NVIR))

    for fetch in fetches:
        fetch.wait()
    line = lax.broadcasted_iota(jnp.int32, (ROWS, NVIR), 0)
    live = jnp.where(line < count[0], rows[OWN, own_part, :].astype(jnp.float32), 0.0)
    rows[OWN, own_part, :] = live.astype(jnp.bfloat16)

    pl.semaphore_wait(barrier, len(everyone))

    first, second = pl.ds(0, SPLIT), pl.ds(SPLIT, NVIR - SPLIT)
    everything = pl.ds(0, NVIR)

    def spread(slot, columns, index, device):
        return start(
            rows.at[OWN, own_part, columns], rows.at[slot, own_part, columns],
            b_send.at[index], b_recv.at[index], device,
        )

    def pass_on(slot, columns, index):
        return start(
            rows.at[slot, own_part, columns], rows.at[slot, own_part, columns],
            b_send.at[index], b_recv.at[index], sibling,
        )

    def to_partner(columns, index):
        return remote(
            rows.at[(1 - lo) * NEXT, own_part, columns], rows.at[MATE, own_part, columns],
            b_send.at[index], b_recv.at[index], partner,
        )

    copies = {}
    copies["own"] = spread(OWN, everything, 0, sibling)
    copies["next a"] = spread(NEXT, first, 1, below)
    copies["next b"] = spread(NEXT, second, 2, below)
    copies["prev"] = spread(PREV, everything, 3, above)
    copies["mate a"] = to_partner(first, 4)
    copies["mate b"] = to_partner(second, 5)

    @pl.when(lo == 1)
    def _():
        copies["mate a"].start()
        copies["mate b"].start()

    def energy(position):
        return occ[pick[position]]

    e_own = energy(blk)
    e_next = energy(y_up * 2 + lo)
    e_prev = energy(y_down * 2 + lo)
    e_mate = energy(((y + lo) % 4) * 2 + 1 - lo)
    pair_energy = (e_own + e_own, e_own + e_next, e_mate + e_own, e_mate + e_prev, e_prev + e_next)
    left = (OWN, OWN, MATE, MATE, PREV)
    right = (OWN, NEXT, OWN, PREV, NEXT)
    turned = y // 2

    def span(which, piece, first=0, size=PIECE):
        return pl.ds(pl.multiple_of(which * HALF + piece * PIECE + first, 16), size)

    def part(piece, first=0, size=PIECE):
        return pl.ds(pl.multiple_of(piece * PIECE + first, 16), size)

    z_up, z_down, z_far = (z + 1) % 4, (z + 3) % 4, (z + 2) % 4
    flip = (core + turned) % 2
    window = pl.ds(pl.multiple_of(flip * (NVIR - WINDOW), 128), WINDOW)

    def at(chunk):
        job, begin, size = CHUNKS[chunk]
        return job, pl.ds(begin, size)

    def cut(chunk):
        return CUTS[TURNS[chunk]]

    def full(chunk, lines):
        job, w = at(chunk)
        if job == 4:
            return half_whole.at[lines, window]
        return whole.at[job, lines, w]

    def turn(slot, index):
        def body(step, carry):
            lines = pl.ds(pl.multiple_of(step * 128, 128), 128)
            flipped[index, :, lines] = jnp.transpose(rows[slot, lines, :].astype(jnp.float32)).astype(jnp.bfloat16)
            return carry

        lax.fori_loop(0, 2 * ROWS // 128, body, 0)

    flip_index = (0, 0, 1, 1, 2)
    arrived = set()

    def need(*names):
        for name in names:
            if name not in arrived:
                arrived.add(name)
                copies[name].wait_recv()

    def own():
        copies["own"].wait_recv()
        turn(OWN, 0)

    def next_a():
        copies["next a"].wait_recv()
        copies["next a on"] = pass_on(NEXT, first, 6)
        pl.when(lo == 0)(copies["mate a"].start)

    def next_b():
        copies["next b"].wait_recv()
        copies["next b on"] = pass_on(NEXT, second, 7)
        pl.when(lo == 0)(copies["mate b"].start)

    def prev():
        copies["prev"].wait_recv()
        copies["prev on"] = pass_on(PREV, everything, 8)

    def turn_prev():
        need("prev on")
        turn(PREV, 2)

    def mate():
        copies["mate a"].wait_recv()
        copies["mate b"].wait_recv()
        copies["mate on"] = pass_on(MATE, everything, 9)

    def turn_mate():
        copies["mate on"].wait_recv()
        turn(MATE, 1)

    def stage0(chunk):
        job, w = at(chunk)
        if job in (1, 4):
            need("next a on")
            if job == 4 or w.start + w.size > SPLIT:
                need("next b on")
        if job == 3:
            need("prev on")
        lhs = flipped[flip_index[job], pl.ds(pl.multiple_of(core * HALF, 16), HALF), :]
        rhs = rows[right[job], :, window] if job == 4 else rows[right[job], :, w]
        partial[job, :, w] = jnp.dot(lhs, rhs, preferred_element_type=jnp.float32).astype(jnp.bfloat16)
        copies[chunk, 0] = start(
            partial.at[job, part(z_far, 0, cut(chunk)), w], z1_up.at[job, pl.ds(0, cut(chunk)), w],
            send.at[chunk, 0], recv.at[chunk, 0], up,
        )
        copies[chunk, 1] = start(
            partial.at[job, part(z_far, cut(chunk), PIECE - cut(chunk)), w],
            z1_down.at[job, pl.ds(0, PIECE - cut(chunk)), w],
            send.at[chunk, 1], recv.at[chunk, 1], down,
        )

    def add(job, w, piece, begin, size, arrived):
        where = part(piece, begin, size)
        partial[job, where, w] = (
            partial[job, where, w].astype(jnp.float32) + arrived[job, 0:size, w].astype(jnp.float32)
        ).astype(jnp.bfloat16)

    def stage1(chunk):
        job, w = at(chunk)
        copies[chunk, 0].wait_recv()
        add(job, w, z_up, 0, cut(chunk), z1_up)
        copies[chunk, 2] = start(
            partial.at[job, part(z_up), w], z2_up.at[job, :, w], send.at[chunk, 2], recv.at[chunk, 2], up
        )
        copies[chunk, 1].wait_recv()
        add(job, w, z_down, cut(chunk), PIECE - cut(chunk), z1_down)
        copies[chunk, 3] = start(
            partial.at[job, part(z_down), w], z2_down.at[job, :, w], send.at[chunk, 3], recv.at[chunk, 3], down
        )

    def stage2(chunk):
        job, w = at(chunk)
        copies[chunk, 2].wait_recv()
        copies[chunk, 3].wait_recv()
        mine[job, :, w] = (
            partial[job, part(z), w].astype(jnp.float32)
            + z2_up[job, :, w].astype(jnp.float32)
            + z2_down[job, :, w].astype(jnp.float32)
        ).astype(jnp.bfloat16)
        copies[chunk, 4] = start(
            mine.at[job, :, w], other.at[job, :, w], send.at[chunk, 4], recv.at[chunk, 4], far
        )

    def same(chunk, lines, index, device):
        copies[chunk, index] = start(
            full(chunk, lines), full(chunk, lines), send.at[chunk, index], recv.at[chunk, index], device
        )

    def stage3(chunk):
        job, w = at(chunk)
        copies[chunk, 4].wait_recv()
        total = (mine[job, :, w].astype(jnp.float32) + other[job, :, w].astype(jnp.float32)).astype(jnp.bfloat16)
        if job == 4:
            half_whole[span(core, z), window] = total
        else:
            whole[job, span(core, z), w] = total
        same(chunk, span(core, z), 5, up)
        same(chunk, span(core, z), 6, down)
        same(chunk, span(core, z), 7, sibling)

    def stage4(chunk):
        copies[chunk, 5].wait_recv()
        same(chunk, span(core, z_down, 0, cut(chunk)), 8, up)
        same(chunk, span(core, z_down), 9, sibling)
        copies[chunk, 6].wait_recv()
        same(chunk, span(core, z_up, cut(chunk), PIECE - cut(chunk)), 10, down)
        same(chunk, span(core, z_up), 11, sibling)

    def stage5(chunk):
        copies[chunk, 8].wait_recv()
        copies[chunk, 10].wait_recv()
        same(chunk, span(core, z_far), 12, sibling)

    def stage6(job):
        for chunk in range(len(CHUNKS)):
            if CHUNKS[chunk][0] == job:
                for index in (7, 9, 11, 12):
                    copies[chunk, index].wait_recv()
        source = half_whole if job == 4 else whole.at[job]
        base = pair_energy[job]

        def body(step, carry):
            lines = pl.ds(pl.multiple_of(step * 128, 128), 128)
            plain = source[lines, :].astype(jnp.float32)
            swapped = jnp.transpose(source[:, lines].astype(jnp.float32))
            gap = (base - virc[lines, 0:1]) - virr[0:1, :]
            value = (2.0 * plain - swapped) / gap
            if job == 4:
                a = lax.broadcasted_iota(jnp.int32, (128, NVIR), 0) + step * 128
                b = lax.broadcasted_iota(jnp.int32, (128, NVIR), 1)
                crossed = (a >= HALF).astype(jnp.int32) + (b >= HALF).astype(jnp.int32)
                value = jnp.where((crossed + turned) % 2 == 0, value, 0.0)
            amp[job, lines, :] = value.astype(jnp.bfloat16)
            return carry

        lax.fori_loop(0, NVIR // 128, body, 0)
        apply(job, first_side[job])

    def stage8(job):
        apply(job, 1 - first_side[job])

    first_side = (0, 1, 0, 0, 1)

    def apply(job, side):
        if side == 0:
            acc[left[job]] = acc[left[job]] + lax.dot_general(
                rows[right[job], own_part, :], amp[job], (((1,), (1,)), ((), ())), preferred_element_type=jnp.float32
            )
        else:
            acc[right[job]] = acc[right[job]] + jnp.dot(
                rows[left[job], own_part, :], amp[job], preferred_element_type=jnp.float32
            )

    def give_back(slot, device):
        index = slot - 1
        back_out[index] = acc[slot].astype(jnp.bfloat16)
        copies[slot] = start(
            back_out.at[index], back_in.at[index], b_send.at[10 + index], b_recv.at[10 + index], device
        )

    own()
    stage0(0)
    stage0(1)
    next_a()
    stage0(2)
    stage1(0)
    prev()
    next_b()
    stage1(2)
    turn_prev()
    stage0(3)
    stage0(8)
    stage1(1)
    stage2(2)
    stage1(3)
    stage1(8)
    mate()
    stage3(2)
    turn_mate()
    stage0(4)
    stage0(5)
    stage0(7)
    stage2(8)
    stage0(6)
    stage1(4)
    stage3(8)
    stage1(6)
    stage1(7)
    stage2(3)
    stage2(4)
    stage4(8)
    stage3(3)
    stage1(5)
    stage2(6)
    stage2(7)
    stage4(2)
    stage2(1)
    stage2(0)
    stage5(8)
    stage4(3)
    stage3(6)
    stage6(4)
    stage2(5)
    stage3(7)
    stage8(4)
    stage5(3)
    stage5(2)
    stage3(4)
    stage4(6)
    stage6(1)
    give_back(NEXT, above)
    stage4(7)
    stage3(5)
    stage5(6)
    stage4(4)
    stage5(7)
    stage8(1)
    stage4(5)
    stage6(3)
    stage3(1)
    stage5(4)
    stage5(5)
    stage3(0)
    stage8(3)
    stage6(2)
    give_back(MATE, giver)
    give_back(PREV, below)
    stage4(0)
    stage4(1)
    stage5(0)
    stage5(1)
    stage6(0)
    stage8(2)
    for slot in (NEXT, PREV, MATE):
        copies[slot].wait_recv()
    total = acc[OWN] + back_in[0].astype(jnp.float32)
    total = total + back_in[1].astype(jnp.float32) + back_in[2].astype(jnp.float32)
    out[...] = total.astype(jnp.bfloat16)
    for copy in started:
        copy.wait_send()


def on_device(b_rows, aux_count, occ_pick, eps_occ, eps_vir):
    bf16, f32 = jnp.bfloat16, jnp.float32
    hbm, vmem = pl.BlockSpec(memory_space=pl.ANY), pl.BlockSpec(memory_space=pltpu.VMEM)
    dma = pltpu.SemaphoreType.DMA
    gamma = pl.pallas_call(
        kernel,
        out_shape=jax.ShapeDtypeStruct((ROWS, NVIR), bf16),
        in_specs=[hbm, hbm, hbm, vmem, hbm],
        out_specs=vmem,
        scratch_shapes=[
            pltpu.SMEM((1,), jnp.int32),
            pltpu.SMEM((8,), jnp.int32),
            pltpu.SMEM((100,), f32),
            dma((4,)),
            pltpu.VMEM((4, 2 * ROWS, NVIR), bf16),
            pltpu.VMEM((3, NVIR, 2 * ROWS), bf16),
            pltpu.VMEM((4, ROWS, NVIR), f32),
            pltpu.VMEM((JOBS, NVIR, NVIR), bf16),
            pltpu.VMEM((NVIR, 128), f32),
            pltpu.VMEM((8, NVIR), f32),
            pltpu.VMEM((JOBS, HALF, NVIR), bf16),
            pltpu.VMEM((JOBS - 1, NVIR, NVIR), bf16),
            pltpu.VMEM((NVIR, NVIR), bf16),
            pltpu.VMEM((JOBS, max(CUTS), NVIR), bf16),
            pltpu.VMEM((JOBS, max(CUTS), NVIR), bf16),
            pltpu.VMEM((JOBS, PIECE, NVIR), bf16),
            pltpu.VMEM((JOBS, PIECE, NVIR), bf16),
            pltpu.VMEM((JOBS, PIECE, NVIR), bf16),
            pltpu.VMEM((JOBS, PIECE, NVIR), bf16),
            pltpu.VMEM((3, ROWS, NVIR), bf16),
            pltpu.VMEM((3, ROWS, NVIR), bf16),
            dma((len(CHUNKS), 13)), dma((len(CHUNKS), 13)), dma((13,)), dma((13,)),
        ],
        compiler_params=pltpu.CompilerParams(
            collective_id=0, has_side_effects=True, vmem_limit_bytes=56 * 2**20
        ),
    )(aux_count, occ_pick, eps_occ, eps_vir, b_rows[:, 0, :])
    return gamma[:, None, :]


def solution(mesh):
    placed = (P("grp", "blk", None), P("grp"), P(), P(), P())
    return jax.shard_map(
        on_device, mesh=mesh, in_specs=placed, out_specs=P("grp", "blk", None), check_vma=False
    )
```

```python
import jax
import jax.numpy as jnp
from jax import lax
from jax.experimental import pallas as pl
from jax.experimental.pallas import tpu as pltpu
from jax.sharding import PartitionSpec as P

MESH = pl.DeviceIdType.MESH
ROWS, NVIR = 320, 896
HALF = NVIR // 2
PIECE = HALF // 4
CUTS = (64, 48)
SPLIT = 512
WINDOW = 512
OWN, NEXT, PREV, MATE = range(4)
JOBS = 5
CHUNKS = ((0, 0, 512), (0, 512, 384), (1, 0, 512), (1, 512, 384), (2, 0, 512), (2, 512, 384), (3, 0, 512), (3, 512, 384), (4, 0, 512))
TURNS = (1, 0, 0, 1, 1, 0, 1, 0, 0)


def device_at(x, y, z, core):
    return (y * 2 + x % 2, z * 4 + (x // 2) * 2 + core)


def kernel(
    count_ref, pick_ref, occ_ref, vir, b_ref, out,
    count, pick, occ, small,
    rows, flipped, acc, amp, virc, virr, partial, whole, half_whole,
    z1_up, z1_down, z2_up, z2_down, mine, other, back_out, back_in,
    send, recv, b_send, b_recv,
):
    blk, grp = lax.axis_index("blk"), lax.axis_index("grp")
    y, lo = blk // 2, blk % 2
    z, core = grp // 4, grp % 2
    x = ((grp // 2) % 2) * 2 + lo
    y_up, y_down = (y + 1) % 4, (y + 3) % 4

    sibling = device_at(x, y, z, 1 - core)
    above, below = device_at(x, y_up, z, core), device_at(x, y_down, z, core)
    partner = device_at(x + 1 - 2 * lo, y, z, core)
    diagonal = device_at(x + 1 - 2 * lo, (y + 3 + 2 * lo) % 4, z, core)
    giver = device_at(x + 1 - 2 * lo, (y + lo) % 4, z, core)
    far = device_at((x + 2) % 4, y, z, core)
    up, down = device_at(x, y, (z + 1) % 4, core), device_at(x, y, (z + 3) % 4, core)

    own_part = pl.ds(pl.multiple_of(core * ROWS, 16), ROWS)
    started = []

    def remote(src, dst, sends, receives, device):
        copy = pltpu.make_async_remote_copy(
            src_ref=src, dst_ref=dst, send_sem=sends, recv_sem=receives,
            device_id=device, device_id_type=MESH,
        )
        started.append(copy)
        return copy

    def start(*where):
        copy = remote(*where)
        copy.start()
        return copy

    fetches = [
        pltpu.make_async_copy(src, dst, small.at[index])
        for index, (src, dst) in enumerate(
            ((b_ref, rows.at[OWN, own_part]), (count_ref, count), (pick_ref, pick), (occ_ref, occ))
        )
    ]
    for fetch in fetches:
        fetch.start()
    half_whole[...] = jnp.zeros_like(half_whole)

    barrier = pltpu.get_barrier_semaphore()
    everyone = (sibling, above, below, partner, diagonal, far, up, down)
    for device in everyone:
        pl.semaphore_signal(barrier, inc=1, device_id=device, device_id_type=MESH)

    acc[...] = jnp.zeros_like(acc)
    virc[...] = jnp.transpose(jnp.broadcast_to(vir[...].reshape(1, NVIR), (128, NVIR)))
    virr[...] = jnp.broadcast_to(vir[...].reshape(1, NVIR), (8, NVIR))

    for fetch in fetches:
        fetch.wait()
    line = lax.broadcasted_iota(jnp.int32, (ROWS, NVIR), 0)
    live = jnp.where(line < count[0], rows[OWN, own_part, :].astype(jnp.float32), 0.0)
    rows[OWN, own_part, :] = live.astype(jnp.bfloat16)

    pl.semaphore_wait(barrier, len(everyone))

    first, second = pl.ds(0, SPLIT), pl.ds(SPLIT, NVIR - SPLIT)
    everything = pl.ds(0, NVIR)

    def spread(slot, columns, index, device):
        return start(
            rows.at[OWN, own_part, columns], rows.at[slot, own_part, columns],
            b_send.at[index], b_recv.at[index], device,
        )

    def pass_on(slot, columns, index):
        return start(
            rows.at[slot, own_part, columns], rows.at[slot, own_part, columns],
            b_send.at[index], b_recv.at[index], sibling,
        )

    def to_partner(columns, index):
        return remote(
            rows.at[(1 - lo) * NEXT, own_part, columns], rows.at[MATE, own_part, columns],
            b_send.at[index], b_recv.at[index], partner,
        )

    copies = {}
    copies["own"] = spread(OWN, everything, 0, sibling)
    copies["next a"] = spread(NEXT, first, 1, below)
    copies["next b"] = spread(NEXT, second, 2, below)
    copies["prev"] = spread(PREV, everything, 3, above)
    copies["mate a"] = to_partner(first, 4)
    copies["mate b"] = to_partner(second, 5)

    @pl.when(lo == 1)
    def _():
        copies["mate a"].start()
        copies["mate b"].start()

    def energy(position):
        return occ[pick[position]]

    e_own = energy(blk)
    e_next = energy(y_up * 2 + lo)
    e_prev = energy(y_down * 2 + lo)
    e_mate = energy(((y + lo) % 4) * 2 + 1 - lo)
    pair_energy = (e_own + e_own, e_own + e_next, e_mate + e_own, e_mate + e_prev, e_prev + e_next)
    left = (OWN, OWN, MATE, MATE, PREV)
    right = (OWN, NEXT, OWN, PREV, NEXT)
    turned = y // 2

    def span(which, piece, first=0, size=PIECE):
        return pl.ds(pl.multiple_of(which * HALF + piece * PIECE + first, 16), size)

    def part(piece, first=0, size=PIECE):
        return pl.ds(pl.multiple_of(piece * PIECE + first, 16), size)

    z_up, z_down, z_far = (z + 1) % 4, (z + 3) % 4, (z + 2) % 4
    flip = (core + turned) % 2
    window = pl.ds(pl.multiple_of(flip * (NVIR - WINDOW), 128), WINDOW)

    def at(chunk):
        job, begin, size = CHUNKS[chunk]
        return job, pl.ds(begin, size)

    def cut(chunk):
        return CUTS[TURNS[chunk]]

    def full(chunk, lines):
        job, w = at(chunk)
        if job == 4:
            return half_whole.at[lines, window]
        return whole.at[job, lines, w]

    def turn(slot, index):
        def body(step, carry):
            lines = pl.ds(pl.multiple_of(step * 128, 128), 128)
            flipped[index, :, lines] = jnp.transpose(rows[slot, lines, :])
            return carry

        lax.fori_loop(0, 2 * ROWS // 128, body, 0, unroll=True)

    flip_index = (0, 0, 1, 1, 2)
    arrived = set()

    def need(*names):
        for name in names:
            if name not in arrived:
                arrived.add(name)
                copies[name].wait_recv()

    def own():
        copies["own"].wait_recv()
        turn(OWN, 0)

    def next_a():
        copies["next a"].wait_recv()
        copies["next a on"] = pass_on(NEXT, first, 6)
        pl.when(lo == 0)(copies["mate a"].start)

    def next_b():
        copies["next b"].wait_recv()
        copies["next b on"] = pass_on(NEXT, second, 7)
        pl.when(lo == 0)(copies["mate b"].start)

    def prev():
        copies["prev"].wait_recv()
        copies["prev on"] = pass_on(PREV, everything, 8)

    def turn_prev():
        need("prev on")
        turn(PREV, 2)

    def mate():
        copies["mate a"].wait_recv()
        copies["mate b"].wait_recv()
        copies["mate on"] = pass_on(MATE, everything, 9)

    def turn_mate():
        copies["mate on"].wait_recv()
        turn(MATE, 1)

    def stage0(chunk):
        job, w = at(chunk)
        if job in (1, 4):
            need("next a on")
            if job == 4 or w.start + w.size > SPLIT:
                need("next b on")
        if job == 3:
            need("prev on")
        lhs = flipped[flip_index[job], pl.ds(pl.multiple_of(core * HALF, 16), HALF), :]
        rhs = rows[right[job], :, window] if job == 4 else rows[right[job], :, w]
        partial[job, :, w] = jnp.dot(lhs, rhs, preferred_element_type=jnp.float32).astype(jnp.bfloat16)
        copies[chunk, 0] = start(
            partial.at[job, part(z_far, 0, cut(chunk)), w], z1_up.at[job, pl.ds(0, cut(chunk)), w],
            send.at[chunk, 0], recv.at[chunk, 0], up,
        )
        copies[chunk, 1] = start(
            partial.at[job, part(z_far, cut(chunk), PIECE - cut(chunk)), w],
            z1_down.at[job, pl.ds(0, PIECE - cut(chunk)), w],
            send.at[chunk, 1], recv.at[chunk, 1], down,
        )

    def add(job, w, piece, begin, size, arrived):
        where = part(piece, begin, size)
        partial[job, where, w] = (
            partial[job, where, w].astype(jnp.float32) + arrived[job, 0:size, w].astype(jnp.float32)
        ).astype(jnp.bfloat16)

    def stage1(chunk):
        job, w = at(chunk)
        copies[chunk, 0].wait_recv()
        add(job, w, z_up, 0, cut(chunk), z1_up)
        copies[chunk, 2] = start(
            partial.at[job, part(z_up), w], z2_up.at[job, :, w], send.at[chunk, 2], recv.at[chunk, 2], up
        )
        copies[chunk, 1].wait_recv()
        add(job, w, z_down, cut(chunk), PIECE - cut(chunk), z1_down)
        copies[chunk, 3] = start(
            partial.at[job, part(z_down), w], z2_down.at[job, :, w], send.at[chunk, 3], recv.at[chunk, 3], down
        )

    def stage2(chunk):
        job, w = at(chunk)
        copies[chunk, 2].wait_recv()
        copies[chunk, 3].wait_recv()
        mine[job, :, w] = (
            partial[job, part(z), w].astype(jnp.float32)
            + z2_up[job, :, w].astype(jnp.float32)
            + z2_down[job, :, w].astype(jnp.float32)
        ).astype(jnp.bfloat16)
        copies[chunk, 4] = start(
            mine.at[job, :, w], other.at[job, :, w], send.at[chunk, 4], recv.at[chunk, 4], far
        )

    def same(chunk, lines, index, device):
        copies[chunk, index] = start(
            full(chunk, lines), full(chunk, lines), send.at[chunk, index], recv.at[chunk, index], device
        )

    def stage3(chunk):
        job, w = at(chunk)
        copies[chunk, 4].wait_recv()
        total = (mine[job, :, w].astype(jnp.float32) + other[job, :, w].astype(jnp.float32)).astype(jnp.bfloat16)
        if job == 4:
            half_whole[span(core, z), window] = total
        else:
            whole[job, span(core, z), w] = total
        same(chunk, span(core, z), 5, up)
        same(chunk, span(core, z), 6, down)
        same(chunk, span(core, z), 7, sibling)

    def stage4(chunk):
        copies[chunk, 5].wait_recv()
        same(chunk, span(core, z_down, 0, cut(chunk)), 8, up)
        same(chunk, span(core, z_down), 9, sibling)
        copies[chunk, 6].wait_recv()
        same(chunk, span(core, z_up, cut(chunk), PIECE - cut(chunk)), 10, down)
        same(chunk, span(core, z_up), 11, sibling)

    def stage5(chunk):
        copies[chunk, 8].wait_recv()
        copies[chunk, 10].wait_recv()
        same(chunk, span(core, z_far), 12, sibling)

    def stage6(job):
        for chunk in range(len(CHUNKS)):
            if CHUNKS[chunk][0] == job:
                for index in (7, 9, 11, 12):
                    copies[chunk, index].wait_recv()
        source = half_whole if job == 4 else whole.at[job]
        base = pair_energy[job]

        def body(step, carry):
            lines = pl.ds(pl.multiple_of(step * 128, 128), 128)
            plain = source[lines, :].astype(jnp.float32)
            swapped = jnp.transpose(source[:, lines]).astype(jnp.float32)
            gap = (base - virc[lines, 0:1]) - virr[0:1, :]
            value = (2.0 * plain - swapped) / gap
            if job == 4:
                a = lax.broadcasted_iota(jnp.int32, (128, NVIR), 0) + step * 128
                b = lax.broadcasted_iota(jnp.int32, (128, NVIR), 1)
                crossed = (a >= HALF).astype(jnp.int32) + (b >= HALF).astype(jnp.int32)
                value = jnp.where((crossed + turned) % 2 == 0, value, 0.0)
            amp[job, lines, :] = value.astype(jnp.bfloat16)
            return carry

        lax.fori_loop(0, NVIR // 128, body, 0, unroll=True)
        apply(job, first_side[job])

    def stage8(job):
        apply(job, 1 - first_side[job])

    first_side = (0, 1, 0, 0, 1)

    def apply(job, side):
        if side == 0:
            acc[left[job]] = acc[left[job]] + lax.dot_general(
                rows[right[job], own_part, :], amp[job], (((1,), (1,)), ((), ())), preferred_element_type=jnp.float32
            )
        else:
            acc[right[job]] = acc[right[job]] + jnp.dot(
                rows[left[job], own_part, :], amp[job], preferred_element_type=jnp.float32
            )

    def give_back(slot, device):
        index = slot - 1
        back_out[index] = acc[slot].astype(jnp.bfloat16)
        copies[slot] = start(
            back_out.at[index], back_in.at[index], b_send.at[10 + index], b_recv.at[10 + index], device
        )

    own()
    stage0(1)
    stage1(1)
    stage0(0)
    next_a()
    stage0(2)
    stage1(0)
    next_b()
    stage1(2)
    prev()
    stage0(3)
    turn_prev()
    stage0(8)
    stage2(2)
    stage1(3)
    stage1(8)
    mate()
    stage2(3)
    stage3(2)
    turn_mate()
    stage2(8)
    stage0(6)
    stage0(4)
    stage2(0)
    stage3(3)
    stage4(2)
    stage0(5)
    stage0(7)
    stage1(6)
    stage1(4)
    stage1(5)
    stage2(6)
    stage3(8)
    stage2(4)
    stage1(7)
    stage4(3)
    stage4(8)
    stage5(2)
    stage2(5)
    stage3(4)
    stage2(7)
    stage5(3)
    stage3(6)
    stage5(8)
    stage6(1)
    stage3(5)
    stage6(4)
    give_back(NEXT, above)
    stage3(7)
    stage2(1)
    stage4(4)
    stage4(5)
    stage4(6)
    stage4(7)
    stage8(4)
    stage5(4)
    stage3(1)
    stage3(0)
    stage5(5)
    stage5(6)
    stage5(7)
    stage6(2)
    stage6(3)
    give_back(MATE, giver)
    stage8(3)
    give_back(PREV, below)
    stage4(1)
    stage8(1)
    stage8(2)
    stage5(1)
    stage4(0)
    stage5(0)
    stage6(0)
    for slot in (NEXT, PREV, MATE):
        copies[slot].wait_recv()
    total = acc[OWN] + back_in[0].astype(jnp.float32)
    total = total + back_in[1].astype(jnp.float32) + back_in[2].astype(jnp.float32)
    out[...] = total.astype(jnp.bfloat16)
    for copy in started:
        copy.wait_send()


def on_device(b_rows, aux_count, occ_pick, eps_occ, eps_vir):
    bf16, f32 = jnp.bfloat16, jnp.float32
    hbm, vmem = pl.BlockSpec(memory_space=pl.ANY), pl.BlockSpec(memory_space=pltpu.VMEM)
    dma = pltpu.SemaphoreType.DMA
    gamma = pl.pallas_call(
        kernel,
        out_shape=jax.ShapeDtypeStruct((ROWS, NVIR), bf16),
        in_specs=[hbm, hbm, hbm, vmem, hbm],
        out_specs=vmem,
        scratch_shapes=[
            pltpu.SMEM((1,), jnp.int32),
            pltpu.SMEM((8,), jnp.int32),
            pltpu.SMEM((100,), f32),
            dma((4,)),
            pltpu.VMEM((4, 2 * ROWS, NVIR), bf16),
            pltpu.VMEM((3, NVIR, 2 * ROWS), bf16),
            pltpu.VMEM((4, ROWS, NVIR), f32),
            pltpu.VMEM((JOBS, NVIR, NVIR), bf16),
            pltpu.VMEM((NVIR, 128), f32),
            pltpu.VMEM((8, NVIR), f32),
            pltpu.VMEM((JOBS, HALF, NVIR), bf16),
            pltpu.VMEM((JOBS - 1, NVIR, NVIR), bf16),
            pltpu.VMEM((NVIR, NVIR), bf16),
            pltpu.VMEM((JOBS, max(CUTS), NVIR), bf16),
            pltpu.VMEM((JOBS, max(CUTS), NVIR), bf16),
            pltpu.VMEM((JOBS, PIECE, NVIR), bf16),
            pltpu.VMEM((JOBS, PIECE, NVIR), bf16),
            pltpu.VMEM((JOBS, PIECE, NVIR), bf16),
            pltpu.VMEM((JOBS, PIECE, NVIR), bf16),
            pltpu.VMEM((3, ROWS, NVIR), bf16),
            pltpu.VMEM((3, ROWS, NVIR), bf16),
            dma((len(CHUNKS), 13)), dma((len(CHUNKS), 13)), dma((13,)), dma((13,)),
        ],
        compiler_params=pltpu.CompilerParams(
            collective_id=0, has_side_effects=True, vmem_limit_bytes=56 * 2**20
        ),
    )(aux_count, occ_pick, eps_occ, eps_vir, b_rows[:, 0, :])
    return gamma[:, None, :]


def solution(mesh):
    placed = (P("grp", "blk", None), P("grp"), P(), P(), P())
    return jax.shard_map(
        on_device, mesh=mesh, in_specs=placed, out_specs=P("grp", "blk", None), check_vma=False
    )
```

```python
import jax
import jax.numpy as jnp
from jax import lax
from jax.experimental import pallas as pl
from jax.experimental.pallas import tpu as pltpu
from jax.sharding import PartitionSpec as P

MESH = pl.DeviceIdType.MESH
ROWS, NVIR = 320, 896
HALF = NVIR // 2
PIECE = HALF // 4
CUTS = (64, 48)
PARTS = ((0, 256), (256, 256), (512, 384))
WINDOW = 512
OWN, NEXT, PREV, MATE = range(4)
JOBS = 5
CHUNKS = ((0, 0, 512), (0, 512, 384), (1, 0, 256), (1, 256, 256), (1, 512, 384), (2, 0, 512), (2, 512, 384), (3, 0, 512), (3, 512, 384), (4, 0, 512))
TURNS = (0, 1, 0, 1, 0, 0, 1, 0, 1, 1)
CROSSED = (5,)


def device_at(x, y, z, core):
    return (y * 2 + x % 2, z * 4 + (x // 2) * 2 + core)


def kernel(
    count_ref, pick_ref, occ_ref, vir, b_ref, out,
    count, pick, occ, small,
    rows, flipped, acc, amp, virc, virr, partial, whole, half_whole,
    z1_up, z1_down, z2_up, z2_down, mine, other, crossing, back_out, back_in,
    send, recv, b_send, b_recv,
):
    blk, grp = lax.axis_index("blk"), lax.axis_index("grp")
    y, lo = blk // 2, blk % 2
    z, core = grp // 4, grp % 2
    x = ((grp // 2) % 2) * 2 + lo
    y_up, y_down = (y + 1) % 4, (y + 3) % 4

    sibling = device_at(x, y, z, 1 - core)
    above, below = device_at(x, y_up, z, core), device_at(x, y_down, z, core)
    partner = device_at(x + 1 - 2 * lo, y, z, core)
    diagonal = device_at(x + 1 - 2 * lo, (y + 3 + 2 * lo) % 4, z, core)
    giver = device_at(x + 1 - 2 * lo, (y + lo) % 4, z, core)
    far = device_at((x + 2) % 4, y, z, core)
    up, down = device_at(x, y, (z + 1) % 4, core), device_at(x, y, (z + 3) % 4, core)

    own_part = pl.ds(pl.multiple_of(core * ROWS, 16), ROWS)
    started = []

    def remote(src, dst, sends, receives, device):
        copy = pltpu.make_async_remote_copy(
            src_ref=src, dst_ref=dst, send_sem=sends, recv_sem=receives,
            device_id=device, device_id_type=MESH,
        )
        started.append(copy)
        return copy

    def start(*where):
        copy = remote(*where)
        copy.start()
        return copy

    fetches = [
        pltpu.make_async_copy(src, dst, small.at[index])
        for index, (src, dst) in enumerate(
            ((b_ref, rows.at[OWN, own_part]), (count_ref, count), (pick_ref, pick), (occ_ref, occ))
        )
    ]
    for fetch in fetches:
        fetch.start()
    half_whole[...] = jnp.zeros_like(half_whole)

    barrier = pltpu.get_barrier_semaphore()
    everyone = (sibling, above, below, partner, diagonal, far, up, down)
    for device in everyone:
        pl.semaphore_signal(barrier, inc=1, device_id=device, device_id_type=MESH)

    acc[...] = jnp.zeros_like(acc)
    virc[...] = jnp.transpose(jnp.broadcast_to(vir[...].reshape(1, NVIR), (128, NVIR)))
    virr[...] = jnp.broadcast_to(vir[...].reshape(1, NVIR), (8, NVIR))

    for fetch in fetches:
        fetch.wait()
    line = lax.broadcasted_iota(jnp.int32, (ROWS, NVIR), 0)
    live = jnp.where(line < count[0], rows[OWN, own_part, :].astype(jnp.float32), 0.0)
    rows[OWN, own_part, :] = live.astype(jnp.bfloat16)

    pl.semaphore_wait(barrier, len(everyone))

    everything = pl.ds(0, NVIR)

    def spread(slot, columns, index, device):
        return start(
            rows.at[OWN, own_part, columns], rows.at[slot, own_part, columns],
            b_send.at[index], b_recv.at[index], device,
        )

    def pass_on(slot, columns, index):
        return start(
            rows.at[slot, own_part, columns], rows.at[slot, own_part, columns],
            b_send.at[index], b_recv.at[index], sibling,
        )

    def to_partner(columns, index):
        return remote(
            rows.at[(1 - lo) * NEXT, own_part, columns], rows.at[MATE, own_part, columns],
            b_send.at[index], b_recv.at[index], partner,
        )

    copies = {}
    pieces = range(len(PARTS))
    copies["own"] = spread(OWN, everything, 0, sibling)
    for i in pieces:
        copies["next", i] = spread(NEXT, pl.ds(*PARTS[i]), 7 + i, below)
    copies["prev"] = spread(PREV, everything, 1, above)
    for i in pieces:
        copies["mate", i] = to_partner(pl.ds(*PARTS[i]), 13 + i)

    @pl.when(lo == 1)
    def _():
        for i in pieces:
            copies["mate", i].start()

    def energy(position):
        return occ[pick[position]]

    e_own = energy(blk)
    e_next = energy(y_up * 2 + lo)
    e_prev = energy(y_down * 2 + lo)
    e_mate = energy(((y + lo) % 4) * 2 + 1 - lo)
    pair_energy = (e_own + e_own, e_own + e_next, e_mate + e_own, e_mate + e_prev, e_prev + e_next)
    left = (OWN, OWN, MATE, MATE, PREV)
    right = (OWN, NEXT, OWN, PREV, NEXT)
    turned = y // 2

    def span(which, piece, first=0, size=PIECE):
        return pl.ds(pl.multiple_of(which * HALF + piece * PIECE + first, 16), size)

    def part(piece, first=0, size=PIECE):
        return pl.ds(pl.multiple_of(piece * PIECE + first, 16), size)

    z_up, z_down, z_far = (z + 1) % 4, (z + 3) % 4, (z + 2) % 4
    flip = (core + turned) % 2
    window = pl.ds(pl.multiple_of(flip * (NVIR - WINDOW), 128), WINDOW)

    side = x // 2

    def at(chunk, of=None):
        job, begin, size = CHUNKS[chunk]
        if chunk not in CROSSED:
            return job, pl.ds(begin, size)
        if of is None:
            of = side
        return job, pl.ds(pl.multiple_of(begin + of * (size // 2), 128), size // 2)

    def cut(chunk):
        return CUTS[TURNS[chunk]]

    def full(chunk, lines, of=None):
        job, w = at(chunk, of)
        if job == 4:
            begin = pl.multiple_of(flip * (NVIR - WINDOW) + w.start, 128)
            return half_whole.at[lines, pl.ds(begin, w.size)]
        return whole.at[job, lines, w]

    def turn(slot, index):
        def body(step, carry):
            lines = pl.ds(pl.multiple_of(step * 128, 128), 128)
            flipped[index, :, lines] = jnp.transpose(rows[slot, lines, :])
            return carry

        lax.fori_loop(0, 2 * ROWS // 128, body, 0, unroll=True)

    flip_index = (0, 0, 1, 1, 2)
    arrived = set()

    def need(*names):
        for name in names:
            if name not in arrived:
                arrived.add(name)
                copies[name].wait_recv()

    def own():
        copies["own"].wait_recv()
        turn(OWN, 0)

    def next_part(i):
        copies["next", i].wait_recv()
        copies["next on", i] = pass_on(NEXT, pl.ds(*PARTS[i]), 10 + i)
        pl.when(lo == 0)(copies["mate", i].start)

    def prev():
        copies["prev"].wait_recv()
        copies["prev on"] = pass_on(PREV, everything, 2)

    def turn_prev():
        need("prev on")
        turn(PREV, 2)

    def mate():
        for i in pieces:
            copies["mate", i].wait_recv()
        copies["mate on"] = pass_on(MATE, everything, 3)

    def turn_mate():
        copies["mate on"].wait_recv()
        turn(MATE, 1)

    def stage0(chunk):
        job, begin, size = CHUNKS[chunk]
        w = pl.ds(begin, size)
        if job in (1, 4):
            for i in pieces:
                if job == 4 or PARTS[i][0] < begin + size:
                    need(("next on", i))
        if job == 3:
            need("prev on")
        lhs = flipped[flip_index[job], pl.ds(pl.multiple_of(core * HALF, 16), HALF), :]
        rhs = rows[right[job], :, window] if job == 4 else rows[right[job], :, w]
        partial[job, :, w] = jnp.dot(lhs, rhs, preferred_element_type=jnp.float32).astype(jnp.bfloat16)
        if chunk in CROSSED:
            copies[chunk, 13] = start(
                partial.at[job, :, at(chunk, 1 - side)[1]], crossing.at[CROSSED.index(chunk)],
                send.at[chunk, 13], recv.at[chunk, 13], far,
            )
        else:
            into_ring(chunk)

    def stage9(chunk):
        job, w = at(chunk)
        copies[chunk, 13].wait_recv()
        partial[job, :, w] = (
            partial[job, :, w].astype(jnp.float32) + crossing[CROSSED.index(chunk)].astype(jnp.float32)
        ).astype(jnp.bfloat16)
        into_ring(chunk)

    def into_ring(chunk):
        job, w = at(chunk)
        copies[chunk, 0] = start(
            partial.at[job, part(z_far, 0, cut(chunk)), w], z1_up.at[job, pl.ds(0, cut(chunk)), w],
            send.at[chunk, 0], recv.at[chunk, 0], up,
        )
        copies[chunk, 1] = start(
            partial.at[job, part(z_far, cut(chunk), PIECE - cut(chunk)), w],
            z1_down.at[job, pl.ds(0, PIECE - cut(chunk)), w],
            send.at[chunk, 1], recv.at[chunk, 1], down,
        )

    def add(job, w, piece, begin, size, arrived):
        where = part(piece, begin, size)
        partial[job, where, w] = (
            partial[job, where, w].astype(jnp.float32) + arrived[job, 0:size, w].astype(jnp.float32)
        ).astype(jnp.bfloat16)

    def stage1(chunk):
        job, w = at(chunk)
        copies[chunk, 0].wait_recv()
        add(job, w, z_up, 0, cut(chunk), z1_up)
        copies[chunk, 2] = start(
            partial.at[job, part(z_up), w], z2_up.at[job, :, w], send.at[chunk, 2], recv.at[chunk, 2], up
        )
        copies[chunk, 1].wait_recv()
        add(job, w, z_down, cut(chunk), PIECE - cut(chunk), z1_down)
        copies[chunk, 3] = start(
            partial.at[job, part(z_down), w], z2_down.at[job, :, w], send.at[chunk, 3], recv.at[chunk, 3], down
        )

    def ring_sum(chunk):
        job, w = at(chunk)
        copies[chunk, 2].wait_recv()
        copies[chunk, 3].wait_recv()
        return (
            partial[job, part(z), w].astype(jnp.float32)
            + z2_up[job, :, w].astype(jnp.float32)
            + z2_down[job, :, w].astype(jnp.float32)
        ).astype(jnp.bfloat16)

    def stage2(chunk):
        job, w = at(chunk)
        mine[job, :, w] = ring_sum(chunk)
        copies[chunk, 4] = start(
            mine.at[job, :, w], other.at[job, :, w], send.at[chunk, 4], recv.at[chunk, 4], far
        )

    def same(chunk, lines, index, device, of=None):
        copies[chunk, index] = start(
            full(chunk, lines, of), full(chunk, lines, of), send.at[chunk, index], recv.at[chunk, index], device
        )

    def both(chunk, lines, index):
        same(chunk, lines, index, sibling)
        if chunk in CROSSED:
            same(chunk, lines, {7: 14, 9: 15, 11: 16, 12: 17}[index], far)

    def stage3(chunk):
        job, w = at(chunk)
        if chunk in CROSSED:
            total = ring_sum(chunk)
        else:
            copies[chunk, 4].wait_recv()
            total = mine[job, :, w].astype(jnp.float32) + other[job, :, w].astype(jnp.float32)
        full(chunk, span(core, z))[...] = total.astype(jnp.bfloat16)
        same(chunk, span(core, z), 5, up)
        same(chunk, span(core, z), 6, down)
        both(chunk, span(core, z), 7)

    def stage4(chunk):
        copies[chunk, 5].wait_recv()
        same(chunk, span(core, z_down, 0, cut(chunk)), 8, up)
        both(chunk, span(core, z_down), 9)
        copies[chunk, 6].wait_recv()
        same(chunk, span(core, z_up, cut(chunk), PIECE - cut(chunk)), 10, down)
        both(chunk, span(core, z_up), 11)

    def stage5(chunk):
        copies[chunk, 8].wait_recv()
        copies[chunk, 10].wait_recv()
        both(chunk, span(core, z_far), 12)

    def stage7(chunk):
        for index in (14, 15, 16, 17):
            copies[chunk, index].wait_recv()
        same(chunk, pl.ds(pl.multiple_of(core * HALF, 16), HALF), 18, sibling, 1 - side)

    def stage6(job):
        for chunk in range(len(CHUNKS)):
            if CHUNKS[chunk][0] == job:
                for index in (7, 9, 11, 12, 18):
                    if index < 18 or chunk in CROSSED:
                        copies[chunk, index].wait_recv()
        source = half_whole if job == 4 else whole.at[job]
        base = pair_energy[job]

        def body(step, carry):
            lines = pl.ds(pl.multiple_of(step * 128, 128), 128)
            plain = source[lines, :].astype(jnp.float32)
            swapped = jnp.transpose(source[:, lines]).astype(jnp.float32)
            gap = (base - virc[lines, 0:1]) - virr[0:1, :]
            value = (2.0 * plain - swapped) / gap
            if job == 4:
                a = lax.broadcasted_iota(jnp.int32, (128, NVIR), 0) + step * 128
                b = lax.broadcasted_iota(jnp.int32, (128, NVIR), 1)
                crossed = (a >= HALF).astype(jnp.int32) + (b >= HALF).astype(jnp.int32)
                value = jnp.where((crossed + turned) % 2 == 0, value, 0.0)
            amp[job, lines, :] = value.astype(jnp.bfloat16)
            return carry

        lax.fori_loop(0, NVIR // 128, body, 0, unroll=True)
        apply(job, first_side[job])

    def stage8(job):
        apply(job, 1 - first_side[job])

    first_side = (0, 1, 0, 0, 1)

    def apply(job, side):
        if side == 0:
            acc[left[job]] = acc[left[job]] + lax.dot_general(
                rows[right[job], own_part, :], amp[job], (((1,), (1,)), ((), ())), preferred_element_type=jnp.float32
            )
        else:
            acc[right[job]] = acc[right[job]] + jnp.dot(
                rows[left[job], own_part, :], amp[job], preferred_element_type=jnp.float32
            )

    def give_back(slot, device):
        index = slot - 1
        back_out[index] = acc[slot].astype(jnp.bfloat16)
        copies[slot] = start(
            back_out.at[index], back_in.at[index], b_send.at[4 + index], b_recv.at[4 + index], device
        )

    own()
    stage0(1)
    next_part(0)
    stage0(2)
    stage0(0)
    stage1(1)
    next_part(1)
    stage1(2)
    stage0(3)
    stage1(0)
    next_part(2)
    stage2(2)
    prev()
    stage0(4)
    stage1(3)
    turn_prev()
    stage0(9)
    stage1(4)
    stage2(3)
    stage3(2)
    mate()
    stage1(9)
    turn_mate()
    stage0(6)
    stage2(4)
    stage0(7)
    stage4(2)
    stage0(5)
    stage3(3)
    stage1(6)
    stage3(4)
    stage1(7)
    stage2(9)
    stage4(3)
    stage9(5)
    stage4(4)
    stage0(8)
    stage2(7)
    stage3(9)
    stage5(3)
    stage1(5)
    stage2(1)
    stage5(4)
    stage1(8)
    stage5(2)
    stage2(6)
    stage4(9)
    stage3(5)
    stage3(7)
    stage6(1)
    stage2(8)
    stage5(9)
    stage4(5)
    stage3(6)
    stage6(4)
    give_back(NEXT, above)
    stage3(8)
    stage5(5)
    stage4(7)
    stage4(6)
    stage8(1)
    stage2(0)
    stage4(8)
    stage7(5)
    stage5(6)
    stage5(7)
    stage3(1)
    stage8(4)
    stage5(8)
    stage6(2)
    stage6(3)
    give_back(MATE, giver)
    stage8(3)
    give_back(PREV, below)
    stage3(0)
    stage4(1)
    stage5(1)
    stage8(2)
    stage4(0)
    stage5(0)
    stage6(0)
    for slot in (NEXT, PREV, MATE):
        copies[slot].wait_recv()
    total = acc[OWN] + back_in[0].astype(jnp.float32)
    total = total + back_in[1].astype(jnp.float32) + back_in[2].astype(jnp.float32)
    out[...] = total.astype(jnp.bfloat16)
    for copy in started:
        copy.wait_send()


def on_device(b_rows, aux_count, occ_pick, eps_occ, eps_vir):
    bf16, f32 = jnp.bfloat16, jnp.float32
    hbm, vmem = pl.BlockSpec(memory_space=pl.ANY), pl.BlockSpec(memory_space=pltpu.VMEM)
    dma = pltpu.SemaphoreType.DMA
    gamma = pl.pallas_call(
        kernel,
        out_shape=jax.ShapeDtypeStruct((ROWS, NVIR), bf16),
        in_specs=[hbm, hbm, hbm, vmem, hbm],
        out_specs=vmem,
        scratch_shapes=[
            pltpu.SMEM((1,), jnp.int32),
            pltpu.SMEM((8,), jnp.int32),
            pltpu.SMEM((100,), f32),
            dma((4,)),
            pltpu.VMEM((4, 2 * ROWS, NVIR), bf16),
            pltpu.VMEM((3, NVIR, 2 * ROWS), bf16),
            pltpu.VMEM((4, ROWS, NVIR), f32),
            pltpu.VMEM((JOBS, NVIR, NVIR), bf16),
            pltpu.VMEM((NVIR, 128), f32),
            pltpu.VMEM((8, NVIR), f32),
            pltpu.VMEM((JOBS, HALF, NVIR), bf16),
            pltpu.VMEM((JOBS - 1, NVIR, NVIR), bf16),
            pltpu.VMEM((NVIR, NVIR), bf16),
            pltpu.VMEM((JOBS, max(CUTS), NVIR), bf16),
            pltpu.VMEM((JOBS, max(CUTS), NVIR), bf16),
            pltpu.VMEM((JOBS, PIECE, NVIR), bf16),
            pltpu.VMEM((JOBS, PIECE, NVIR), bf16),
            pltpu.VMEM((JOBS, PIECE, NVIR), bf16),
            pltpu.VMEM((JOBS, PIECE, NVIR), bf16),
            pltpu.VMEM((max(1, len(CROSSED)), HALF, 256), bf16),
            pltpu.VMEM((3, ROWS, NVIR), bf16),
            pltpu.VMEM((3, ROWS, NVIR), bf16),
            dma((len(CHUNKS), 19)), dma((len(CHUNKS), 19)), dma((16,)), dma((16,)),
        ],
        compiler_params=pltpu.CompilerParams(
            collective_id=0, has_side_effects=True, vmem_limit_bytes=56 * 2**20
        ),
    )(aux_count, occ_pick, eps_occ, eps_vir, b_rows[:, 0, :])
    return gamma[:, None, :]


def solution(mesh):
    placed = (P("grp", "blk", None), P("grp"), P(), P(), P())
    return jax.shard_map(
        on_device, mesh=mesh, in_specs=placed, out_specs=P("grp", "blk", None), check_vma=False
    )
```

```python
import jax
import jax.numpy as jnp
from jax import lax
from jax.experimental import pallas as pl
from jax.experimental.pallas import tpu as pltpu
from jax.sharding import PartitionSpec as P

MESH = pl.DeviceIdType.MESH
ROWS, NVIR = 320, 896
HALF = NVIR // 2
PIECE = HALF // 4
CUTS = (64, 48)
PARTS = ((0, 256), (256, 256), (512, 384))
WINDOW = 512
OWN, NEXT, PREV, MATE = range(4)
JOBS = 5
CHUNKS = ((0, 0, 512), (0, 512, 384), (1, 0, 256), (1, 256, 256), (1, 512, 384), (2, 0, 512), (2, 512, 384), (3, 0, 512), (3, 512, 384), (4, 0, 512))
TURNS = (0, 1, 0, 1, 0, 0, 1, 0, 1, 1)
CROSSED = (5,)


def device_at(x, y, z, core):
    return (y * 2 + x % 2, z * 4 + (x // 2) * 2 + core)


def kernel(
    count_ref, pick_ref, occ_ref, vir, b_ref, out,
    count, pick, occ, small,
    rows, flipped, acc, amp, virc, virr, partial, whole, half_whole,
    z1_up, z1_down, z2_up, z2_down, mine, other, crossing, back_out, back_in, result,
    send, recv, b_send, b_recv,
):
    blk, grp = lax.axis_index("blk"), lax.axis_index("grp")
    y, lo = blk // 2, blk % 2
    z, core = grp // 4, grp % 2
    x = ((grp // 2) % 2) * 2 + lo
    y_up, y_down = (y + 1) % 4, (y + 3) % 4

    sibling = device_at(x, y, z, 1 - core)
    above, below = device_at(x, y_up, z, core), device_at(x, y_down, z, core)
    partner = device_at(x + 1 - 2 * lo, y, z, core)
    diagonal = device_at(x + 1 - 2 * lo, (y + 3 + 2 * lo) % 4, z, core)
    giver = device_at(x + 1 - 2 * lo, (y + lo) % 4, z, core)
    far = device_at((x + 2) % 4, y, z, core)
    up, down = device_at(x, y, (z + 1) % 4, core), device_at(x, y, (z + 3) % 4, core)

    own_part = pl.ds(pl.multiple_of(core * ROWS, 16), ROWS)
    started = []

    def remote(src, dst, sends, receives, device):
        copy = pltpu.make_async_remote_copy(
            src_ref=src, dst_ref=dst, send_sem=sends, recv_sem=receives,
            device_id=device, device_id_type=MESH,
        )
        started.append(copy)
        return copy

    def start(*where):
        copy = remote(*where)
        copy.start()
        return copy

    fetches = [
        pltpu.make_async_copy(src, dst, small.at[index])
        for index, (src, dst) in enumerate(
            ((b_ref, rows.at[OWN, own_part]), (count_ref, count), (pick_ref, pick), (occ_ref, occ))
        )
    ]
    for fetch in fetches:
        fetch.start()
    half_whole[...] = jnp.zeros_like(half_whole)

    barrier = pltpu.get_barrier_semaphore()
    everyone = (sibling, above, below, partner, diagonal, far, up, down)
    for device in everyone:
        pl.semaphore_signal(barrier, inc=1, device_id=device, device_id_type=MESH)

    acc[...] = jnp.zeros_like(acc)
    virc[...] = jnp.transpose(jnp.broadcast_to(vir[...].reshape(1, NVIR), (128, NVIR)))
    virr[...] = jnp.broadcast_to(vir[...].reshape(1, NVIR), (8, NVIR))

    for fetch in fetches:
        fetch.wait()
    line = lax.broadcasted_iota(jnp.int32, (ROWS, NVIR), 0)
    live = jnp.where(line < count[0], rows[OWN, own_part, :].astype(jnp.float32), 0.0)
    rows[OWN, own_part, :] = live.astype(jnp.bfloat16)

    pl.semaphore_wait(barrier, len(everyone))

    everything = pl.ds(0, NVIR)

    def spread(slot, columns, index, device):
        return start(
            rows.at[OWN, own_part, columns], rows.at[slot, own_part, columns],
            b_send.at[index], b_recv.at[index], device,
        )

    def pass_on(slot, columns, index):
        return start(
            rows.at[slot, own_part, columns], rows.at[slot, own_part, columns],
            b_send.at[index], b_recv.at[index], sibling,
        )

    def to_partner(columns, index):
        return remote(
            rows.at[(1 - lo) * NEXT, own_part, columns], rows.at[MATE, own_part, columns],
            b_send.at[index], b_recv.at[index], partner,
        )

    copies = {}
    pieces = range(len(PARTS))
    copies["own"] = spread(OWN, everything, 0, sibling)
    for i in pieces:
        copies["next", i] = spread(NEXT, pl.ds(*PARTS[i]), 10 + i, below)
    copies["prev"] = spread(PREV, everything, 1, above)
    for i in pieces:
        copies["mate", i] = to_partner(pl.ds(*PARTS[i]), 16 + i)

    @pl.when(lo == 1)
    def _():
        for i in pieces:
            copies["mate", i].start()

    def energy(position):
        return occ[pick[position]]

    e_own = energy(blk)
    e_next = energy(y_up * 2 + lo)
    e_prev = energy(y_down * 2 + lo)
    e_mate = energy(((y + lo) % 4) * 2 + 1 - lo)
    pair_energy = (e_own + e_own, e_own + e_next, e_mate + e_own, e_mate + e_prev, e_prev + e_next)
    left = (OWN, OWN, MATE, MATE, PREV)
    right = (OWN, NEXT, OWN, PREV, NEXT)
    turned = y // 2

    def span(which, piece, first=0, size=PIECE):
        return pl.ds(pl.multiple_of(which * HALF + piece * PIECE + first, 16), size)

    def part(piece, first=0, size=PIECE):
        return pl.ds(pl.multiple_of(piece * PIECE + first, 16), size)

    z_up, z_down, z_far = (z + 1) % 4, (z + 3) % 4, (z + 2) % 4
    flip = (core + turned) % 2
    window = pl.ds(pl.multiple_of(flip * (NVIR - WINDOW), 128), WINDOW)

    side = x // 2

    def at(chunk, of=None):
        job, begin, size = CHUNKS[chunk]
        if chunk not in CROSSED:
            return job, pl.ds(begin, size)
        if of is None:
            of = side
        return job, pl.ds(pl.multiple_of(begin + of * (size // 2), 128), size // 2)

    def cut(chunk):
        return CUTS[TURNS[chunk]]

    def full(chunk, lines, of=None):
        job, w = at(chunk, of)
        if job == 4:
            begin = pl.multiple_of(flip * (NVIR - WINDOW) + w.start, 128)
            return half_whole.at[lines, pl.ds(begin, w.size)]
        return whole.at[job, lines, w]

    def turn(slot, index):
        def body(step, carry):
            lines = pl.ds(pl.multiple_of(step * 128, 128), 128)
            flipped[index, :, lines] = jnp.transpose(rows[slot, lines, :])
            return carry

        lax.fori_loop(0, 2 * ROWS // 128, body, 0, unroll=True)

    flip_index = (0, 0, 1, 1, 2)
    arrived = set()

    def need(*names):
        for name in names:
            if name not in arrived:
                arrived.add(name)
                copies[name].wait_recv()

    def own():
        copies["own"].wait_recv()
        turn(OWN, 0)

    def next_part(i):
        copies["next", i].wait_recv()
        copies["next on", i] = pass_on(NEXT, pl.ds(*PARTS[i]), 13 + i)
        pl.when(lo == 0)(copies["mate", i].start)

    def prev():
        copies["prev"].wait_recv()
        copies["prev on"] = pass_on(PREV, everything, 2)

    def turn_prev():
        need("prev on")
        turn(PREV, 2)

    def mate():
        for i in pieces:
            copies["mate", i].wait_recv()
        copies["mate on"] = pass_on(MATE, everything, 3)

    def turn_mate():
        copies["mate on"].wait_recv()
        turn(MATE, 1)

    def stage0(chunk):
        job, begin, size = CHUNKS[chunk]
        w = pl.ds(begin, size)
        if job in (1, 4):
            for i in pieces:
                if job == 4 or PARTS[i][0] < begin + size:
                    need(("next on", i))
        if job == 3:
            need("prev on")
        lhs = flipped[flip_index[job], pl.ds(pl.multiple_of(core * HALF, 16), HALF), :]
        rhs = rows[right[job], :, window] if job == 4 else rows[right[job], :, w]
        partial[job, :, w] = jnp.dot(lhs, rhs, preferred_element_type=jnp.float32).astype(jnp.bfloat16)
        if chunk in CROSSED:
            copies[chunk, 13] = start(
                partial.at[job, :, at(chunk, 1 - side)[1]], crossing.at[CROSSED.index(chunk)],
                send.at[chunk, 13], recv.at[chunk, 13], far,
            )
        else:
            into_ring(chunk)

    def stage9(chunk):
        job, w = at(chunk)
        copies[chunk, 13].wait_recv()
        partial[job, :, w] = (
            partial[job, :, w].astype(jnp.float32) + crossing[CROSSED.index(chunk)].astype(jnp.float32)
        ).astype(jnp.bfloat16)
        into_ring(chunk)

    def into_ring(chunk):
        job, w = at(chunk)
        copies[chunk, 0] = start(
            partial.at[job, part(z_far, 0, cut(chunk)), w], z1_up.at[job, pl.ds(0, cut(chunk)), w],
            send.at[chunk, 0], recv.at[chunk, 0], up,
        )
        copies[chunk, 1] = start(
            partial.at[job, part(z_far, cut(chunk), PIECE - cut(chunk)), w],
            z1_down.at[job, pl.ds(0, PIECE - cut(chunk)), w],
            send.at[chunk, 1], recv.at[chunk, 1], down,
        )

    def add(job, w, piece, begin, size, arrived):
        where = part(piece, begin, size)
        partial[job, where, w] = (
            partial[job, where, w].astype(jnp.float32) + arrived[job, 0:size, w].astype(jnp.float32)
        ).astype(jnp.bfloat16)

    def stage1(chunk):
        job, w = at(chunk)
        copies[chunk, 0].wait_recv()
        add(job, w, z_up, 0, cut(chunk), z1_up)
        copies[chunk, 2] = start(
            partial.at[job, part(z_up), w], z2_up.at[job, :, w], send.at[chunk, 2], recv.at[chunk, 2], up
        )
        copies[chunk, 1].wait_recv()
        add(job, w, z_down, cut(chunk), PIECE - cut(chunk), z1_down)
        copies[chunk, 3] = start(
            partial.at[job, part(z_down), w], z2_down.at[job, :, w], send.at[chunk, 3], recv.at[chunk, 3], down
        )

    def ring_sum(chunk):
        job, w = at(chunk)
        copies[chunk, 2].wait_recv()
        copies[chunk, 3].wait_recv()
        return (
            partial[job, part(z), w].astype(jnp.float32)
            + z2_up[job, :, w].astype(jnp.float32)
            + z2_down[job, :, w].astype(jnp.float32)
        ).astype(jnp.bfloat16)

    def stage2(chunk):
        job, w = at(chunk)
        mine[job, :, w] = ring_sum(chunk)
        copies[chunk, 4] = start(
            mine.at[job, :, w], other.at[job, :, w], send.at[chunk, 4], recv.at[chunk, 4], far
        )

    def same(chunk, lines, index, device, of=None):
        copies[chunk, index] = start(
            full(chunk, lines, of), full(chunk, lines, of), send.at[chunk, index], recv.at[chunk, index], device
        )

    def both(chunk, lines, index):
        same(chunk, lines, index, sibling)
        if chunk in CROSSED:
            same(chunk, lines, {7: 14, 9: 15, 11: 16, 12: 17}[index], far)

    def stage3(chunk):
        job, w = at(chunk)
        if chunk in CROSSED:
            total = ring_sum(chunk)
        else:
            copies[chunk, 4].wait_recv()
            total = mine[job, :, w].astype(jnp.float32) + other[job, :, w].astype(jnp.float32)
        full(chunk, span(core, z))[...] = total.astype(jnp.bfloat16)
        same(chunk, span(core, z), 5, up)
        same(chunk, span(core, z), 6, down)
        both(chunk, span(core, z), 7)

    def stage4(chunk):
        copies[chunk, 5].wait_recv()
        same(chunk, span(core, z_down, 0, cut(chunk)), 8, up)
        both(chunk, span(core, z_down), 9)
        copies[chunk, 6].wait_recv()
        same(chunk, span(core, z_up, cut(chunk), PIECE - cut(chunk)), 10, down)
        both(chunk, span(core, z_up), 11)

    def stage5(chunk):
        copies[chunk, 8].wait_recv()
        copies[chunk, 10].wait_recv()
        both(chunk, span(core, z_far), 12)

    def stage7(chunk):
        for index in (14, 15, 16, 17):
            copies[chunk, index].wait_recv()
        same(chunk, pl.ds(pl.multiple_of(core * HALF, 16), HALF), 18, sibling, 1 - side)

    def stage6(job):
        for chunk in range(len(CHUNKS)):
            if CHUNKS[chunk][0] == job:
                for index in (7, 9, 11, 12, 18):
                    if index < 18 or chunk in CROSSED:
                        copies[chunk, index].wait_recv()
        source = half_whole if job == 4 else whole.at[job]
        base = pair_energy[job]

        def body(step, carry):
            lines = pl.ds(pl.multiple_of(step * 128, 128), 128)
            plain = source[lines, :].astype(jnp.float32)
            swapped = jnp.transpose(source[:, lines]).astype(jnp.float32)
            gap = (base - virc[lines, 0:1]) - virr[0:1, :]
            value = (2.0 * plain - swapped) / gap
            if job == 4:
                a = lax.broadcasted_iota(jnp.int32, (128, NVIR), 0) + step * 128
                b = lax.broadcasted_iota(jnp.int32, (128, NVIR), 1)
                crossed = (a >= HALF).astype(jnp.int32) + (b >= HALF).astype(jnp.int32)
                value = jnp.where((crossed + turned) % 2 == 0, value, 0.0)
            amp[job, lines, :] = value.astype(jnp.bfloat16)
            return carry

        lax.fori_loop(0, NVIR // 128, body, 0, unroll=True)
        apply(job, first_side[job])

    def stage8(job):
        apply(job, 1 - first_side[job])

    first_side = (0, 1, 0, 0, 1)

    def apply(job, side):
        if side == 0:
            acc[left[job]] = acc[left[job]] + lax.dot_general(
                rows[right[job], own_part, :], amp[job], (((1,), (1,)), ((), ())), preferred_element_type=jnp.float32
            )
        else:
            acc[right[job]] = acc[right[job]] + jnp.dot(
                rows[left[job], own_part, :], amp[job], preferred_element_type=jnp.float32
            )

    halves = (pl.ds(0, ROWS // 2), pl.ds(ROWS // 2, ROWS // 2))

    def give_back(slot, device):
        index = slot - 1
        for h, lines in enumerate(halves):
            back_out[index, lines, :] = acc[slot, lines, :].astype(jnp.bfloat16)
            copies[slot, h] = start(
                back_out.at[index, lines], back_in.at[index, lines],
                b_send.at[4 + 2 * index + h], b_recv.at[4 + 2 * index + h], device,
            )

    own()
    stage0(1)
    stage0(0)
    next_part(0)
    stage1(1)
    stage0(2)
    stage1(0)
    next_part(1)
    stage0(3)
    stage1(2)
    next_part(2)
    stage1(3)
    prev()
    stage2(2)
    stage0(4)
    turn_prev()
    stage2(3)
    stage0(9)
    stage1(4)
    stage3(2)
    stage3(3)
    stage2(4)
    stage1(9)
    mate()
    stage4(2)
    stage4(3)
    turn_mate()
    stage0(6)
    stage0(7)
    stage0(5)
    stage3(4)
    stage0(8)
    stage1(7)
    stage1(6)
    stage2(9)
    stage1(8)
    stage9(5)
    stage2(7)
    stage5(2)
    stage2(0)
    stage3(9)
    stage2(6)
    stage1(5)
    stage4(4)
    stage2(8)
    stage4(9)
    stage2(1)
    stage3(5)
    stage5(3)
    stage5(4)
    stage3(7)
    stage5(9)
    stage3(6)
    stage6(1)
    stage4(5)
    stage6(4)
    give_back(NEXT, above)
    stage8(4)
    stage3(8)
    stage5(5)
    stage4(6)
    stage4(7)
    stage4(8)
    stage5(6)
    stage7(5)
    stage5(7)
    stage5(8)
    stage3(0)
    stage6(2)
    stage6(3)
    give_back(MATE, giver)
    stage8(3)
    give_back(PREV, below)
    stage8(1)
    stage4(0)
    stage3(1)
    stage5(0)
    stage4(1)
    stage5(1)
    stage8(2)
    stage6(0)
    stores = []
    for h, lines in enumerate(halves):
        for slot in (NEXT, PREV, MATE):
            copies[slot, h].wait_recv()
        total = acc[OWN, lines, :] + back_in[0, lines, :].astype(jnp.float32)
        total = total + back_in[1, lines, :].astype(jnp.float32) + back_in[2, lines, :].astype(jnp.float32)
        result[lines, :] = total.astype(jnp.bfloat16)
        stores.append(pltpu.make_async_copy(result.at[lines], out.at[lines], small.at[4 + h]))
        stores[h].start()
    for store in stores:
        store.wait()
    for copy in started:
        copy.wait_send()


def on_device(b_rows, aux_count, occ_pick, eps_occ, eps_vir):
    bf16, f32 = jnp.bfloat16, jnp.float32
    hbm, vmem = pl.BlockSpec(memory_space=pl.ANY), pl.BlockSpec(memory_space=pltpu.VMEM)
    dma = pltpu.SemaphoreType.DMA
    gamma = pl.pallas_call(
        kernel,
        out_shape=jax.ShapeDtypeStruct((ROWS, NVIR), bf16),
        in_specs=[hbm, hbm, hbm, vmem, hbm],
        out_specs=hbm,
        scratch_shapes=[
            pltpu.SMEM((1,), jnp.int32),
            pltpu.SMEM((8,), jnp.int32),
            pltpu.SMEM((100,), f32),
            dma((6,)),
            pltpu.VMEM((4, 2 * ROWS, NVIR), bf16),
            pltpu.VMEM((3, NVIR, 2 * ROWS), bf16),
            pltpu.VMEM((4, ROWS, NVIR), f32),
            pltpu.VMEM((JOBS, NVIR, NVIR), bf16),
            pltpu.VMEM((NVIR, 128), f32),
            pltpu.VMEM((8, NVIR), f32),
            pltpu.VMEM((JOBS, HALF, NVIR), bf16),
            pltpu.VMEM((JOBS - 1, NVIR, NVIR), bf16),
            pltpu.VMEM((NVIR, NVIR), bf16),
            pltpu.VMEM((JOBS, max(CUTS), NVIR), bf16),
            pltpu.VMEM((JOBS, max(CUTS), NVIR), bf16),
            pltpu.VMEM((JOBS, PIECE, NVIR), bf16),
            pltpu.VMEM((JOBS, PIECE, NVIR), bf16),
            pltpu.VMEM((JOBS, PIECE, NVIR), bf16),
            pltpu.VMEM((JOBS, PIECE, NVIR), bf16),
            pltpu.VMEM((max(1, len(CROSSED)), HALF, 256), bf16),
            pltpu.VMEM((3, ROWS, NVIR), bf16),
            pltpu.VMEM((3, ROWS, NVIR), bf16),
            pltpu.VMEM((ROWS, NVIR), bf16),
            dma((len(CHUNKS), 19)), dma((len(CHUNKS), 19)), dma((19,)), dma((19,)),
        ],
        compiler_params=pltpu.CompilerParams(
            collective_id=0, has_side_effects=True, vmem_limit_bytes=56 * 2**20
        ),
    )(aux_count, occ_pick, eps_occ, eps_vir, b_rows[:, 0, :])
    return gamma[:, None, :]


def solution(mesh):
    placed = (P("grp", "blk", None), P("grp"), P(), P(), P())
    return jax.shard_map(
        on_device, mesh=mesh, in_specs=placed, out_specs=P("grp", "blk", None), check_vma=False
    )
```

```python
import jax
import jax.numpy as jnp
from jax import lax
from jax.experimental import pallas as pl
from jax.experimental.pallas import tpu as pltpu
from jax.sharding import PartitionSpec as P

MESH = pl.DeviceIdType.MESH
ROWS, NVIR = 320, 896
HALF = NVIR // 2
PIECE = HALF // 4
CUTS = (64, 48)
PARTS = ((0, 256), (256, 256), (512, 384))
WINDOW = 512
OWN, NEXT, PREV, MATE = range(4)
JOBS = 5
CHUNKS = ((0, 0, 512), (0, 512, 384), (1, 0, 256), (1, 256, 256), (1, 512, 384), (2, 0, 512), (2, 512, 384), (3, 0, 512), (3, 512, 384), (4, 0, 512))
TURNS = (0, 1, 0, 1, 0, 0, 1, 0, 1, 1)
CROSSED = (5,)


def device_at(x, y, z, core):
    return (y * 2 + x % 2, z * 4 + (x // 2) * 2 + core)


def kernel(
    count_ref, pick_ref, occ_ref, vir_ref, b_ref, out,
    count, pick, occ, vir, small,
    rows, flipped, acc, amp, virc, virr, partial, whole, half_whole,
    z1_up, z1_down, z2_up, z2_down, mine, other, crossing, back_out, back_in, result,
    send, recv, b_send, b_recv,
):
    blk, grp = lax.axis_index("blk"), lax.axis_index("grp")
    y, lo = blk // 2, blk % 2
    z, core = grp // 4, grp % 2
    x = ((grp // 2) % 2) * 2 + lo
    y_up, y_down = (y + 1) % 4, (y + 3) % 4

    sibling = device_at(x, y, z, 1 - core)
    above, below = device_at(x, y_up, z, core), device_at(x, y_down, z, core)
    partner = device_at(x + 1 - 2 * lo, y, z, core)
    diagonal = device_at(x + 1 - 2 * lo, (y + 3 + 2 * lo) % 4, z, core)
    giver = device_at(x + 1 - 2 * lo, (y + lo) % 4, z, core)
    far = device_at((x + 2) % 4, y, z, core)
    up, down = device_at(x, y, (z + 1) % 4, core), device_at(x, y, (z + 3) % 4, core)

    own_part = pl.ds(pl.multiple_of(core * ROWS, 16), ROWS)
    started = []

    def remote(src, dst, sends, receives, device):
        copy = pltpu.make_async_remote_copy(
            src_ref=src, dst_ref=dst, send_sem=sends, recv_sem=receives,
            device_id=device, device_id_type=MESH,
        )
        started.append(copy)
        return copy

    def start(*where):
        copy = remote(*where)
        copy.start()
        return copy

    barrier = pltpu.get_barrier_semaphore()
    everyone = (sibling, above, below, partner, diagonal, far, up, down)
    for device in everyone:
        pl.semaphore_signal(barrier, inc=1, device_id=device, device_id_type=MESH)

    fetches = [
        pltpu.make_async_copy(src, dst, small.at[index])
        for index, (src, dst) in enumerate(
            (
                (b_ref, rows.at[OWN, own_part]), (count_ref, count), (vir_ref, vir),
                (pick_ref, pick), (occ_ref, occ),
            )
        )
    ]
    for fetch in fetches:
        fetch.start()

    half_whole[...] = jnp.zeros_like(half_whole)
    acc[...] = jnp.zeros_like(acc)

    fetches[0].wait()
    fetches[1].wait()
    line = lax.broadcasted_iota(jnp.int32, (ROWS, NVIR), 0)
    live = jnp.where(line < count[0], rows[OWN, own_part, :].astype(jnp.float32), 0.0)
    rows[OWN, own_part, :] = live.astype(jnp.bfloat16)

    pl.semaphore_wait(barrier, len(everyone))

    everything = pl.ds(0, NVIR)

    def spread(slot, columns, index, device):
        return start(
            rows.at[OWN, own_part, columns], rows.at[slot, own_part, columns],
            b_send.at[index], b_recv.at[index], device,
        )

    def pass_on(slot, columns, index):
        return start(
            rows.at[slot, own_part, columns], rows.at[slot, own_part, columns],
            b_send.at[index], b_recv.at[index], sibling,
        )

    def to_partner(columns, index):
        return remote(
            rows.at[(1 - lo) * NEXT, own_part, columns], rows.at[MATE, own_part, columns],
            b_send.at[index], b_recv.at[index], partner,
        )

    copies = {}
    pieces = range(len(PARTS))
    copies["own"] = spread(OWN, everything, 0, sibling)
    for i in pieces:
        copies["next", i] = spread(NEXT, pl.ds(*PARTS[i]), 10 + i, below)
    copies["prev"] = spread(PREV, everything, 1, above)
    for i in pieces:
        copies["mate", i] = to_partner(pl.ds(*PARTS[i]), 16 + i)

    @pl.when(lo == 1)
    def _():
        for i in pieces:
            copies["mate", i].start()

    for fetch in fetches[2:]:
        fetch.wait()
    virc[...] = jnp.transpose(jnp.broadcast_to(vir[...].reshape(1, NVIR), (128, NVIR)))
    virr[...] = jnp.broadcast_to(vir[...].reshape(1, NVIR), (8, NVIR))

    def energy(position):
        return occ[pick[position]]

    e_own = energy(blk)
    e_next = energy(y_up * 2 + lo)
    e_prev = energy(y_down * 2 + lo)
    e_mate = energy(((y + lo) % 4) * 2 + 1 - lo)
    pair_energy = (e_own + e_own, e_own + e_next, e_mate + e_own, e_mate + e_prev, e_prev + e_next)
    left = (OWN, OWN, MATE, MATE, PREV)
    right = (OWN, NEXT, OWN, PREV, NEXT)
    turned = y // 2

    def span(which, piece, first=0, size=PIECE):
        return pl.ds(pl.multiple_of(which * HALF + piece * PIECE + first, 16), size)

    def part(piece, first=0, size=PIECE):
        return pl.ds(pl.multiple_of(piece * PIECE + first, 16), size)

    z_up, z_down, z_far = (z + 1) % 4, (z + 3) % 4, (z + 2) % 4
    flip = (core + turned) % 2
    window = pl.ds(pl.multiple_of(flip * (NVIR - WINDOW), 128), WINDOW)

    side = x // 2

    def at(chunk, of=None):
        job, begin, size = CHUNKS[chunk]
        if chunk not in CROSSED:
            return job, pl.ds(begin, size)
        if of is None:
            of = side
        return job, pl.ds(pl.multiple_of(begin + of * (size // 2), 128), size // 2)

    def cut(chunk):
        return CUTS[TURNS[chunk]]

    def full(chunk, lines, of=None):
        job, w = at(chunk, of)
        if job == 4:
            begin = pl.multiple_of(flip * (NVIR - WINDOW) + w.start, 128)
            return half_whole.at[lines, pl.ds(begin, w.size)]
        return whole.at[job, lines, w]

    def turn(slot, index):
        def body(step, carry):
            lines = pl.ds(pl.multiple_of(step * 128, 128), 128)
            flipped[index, :, lines] = jnp.transpose(rows[slot, lines, :])
            return carry

        lax.fori_loop(0, 2 * ROWS // 128, body, 0, unroll=True)

    flip_index = (0, 0, 1, 1, 2)
    arrived = set()

    def need(*names):
        for name in names:
            if name not in arrived:
                arrived.add(name)
                copies[name].wait_recv()

    def own():
        copies["own"].wait_recv()
        turn(OWN, 0)

    def next_part(i):
        copies["next", i].wait_recv()
        copies["next on", i] = pass_on(NEXT, pl.ds(*PARTS[i]), 13 + i)
        pl.when(lo == 0)(copies["mate", i].start)

    def prev():
        copies["prev"].wait_recv()
        copies["prev on"] = pass_on(PREV, everything, 2)

    def turn_prev():
        need("prev on")
        turn(PREV, 2)

    def mate():
        for i in pieces:
            copies["mate", i].wait_recv()
        copies["mate on"] = pass_on(MATE, everything, 3)

    def turn_mate():
        copies["mate on"].wait_recv()
        turn(MATE, 1)

    def stage0(chunk):
        job, begin, size = CHUNKS[chunk]
        w = pl.ds(begin, size)
        if job in (1, 4):
            for i in pieces:
                if job == 4 or PARTS[i][0] < begin + size:
                    need(("next on", i))
        if job == 3:
            need("prev on")
        lhs = flipped[flip_index[job], pl.ds(pl.multiple_of(core * HALF, 16), HALF), :]
        rhs = rows[right[job], :, window] if job == 4 else rows[right[job], :, w]
        partial[job, :, w] = jnp.dot(lhs, rhs, preferred_element_type=jnp.float32).astype(jnp.bfloat16)
        if chunk in CROSSED:
            copies[chunk, 13] = start(
                partial.at[job, :, at(chunk, 1 - side)[1]], crossing.at[CROSSED.index(chunk)],
                send.at[chunk, 13], recv.at[chunk, 13], far,
            )
        else:
            into_ring(chunk)

    def stage9(chunk):
        job, w = at(chunk)
        copies[chunk, 13].wait_recv()
        partial[job, :, w] = (
            partial[job, :, w].astype(jnp.float32) + crossing[CROSSED.index(chunk)].astype(jnp.float32)
        ).astype(jnp.bfloat16)
        into_ring(chunk)

    def into_ring(chunk):
        job, w = at(chunk)
        copies[chunk, 0] = start(
            partial.at[job, part(z_far, 0, cut(chunk)), w], z1_up.at[job, pl.ds(0, cut(chunk)), w],
            send.at[chunk, 0], recv.at[chunk, 0], up,
        )
        copies[chunk, 1] = start(
            partial.at[job, part(z_far, cut(chunk), PIECE - cut(chunk)), w],
            z1_down.at[job, pl.ds(0, PIECE - cut(chunk)), w],
            send.at[chunk, 1], recv.at[chunk, 1], down,
        )

    def add(job, w, piece, begin, size, arrived):
        where = part(piece, begin, size)
        partial[job, where, w] = (
            partial[job, where, w].astype(jnp.float32) + arrived[job, 0:size, w].astype(jnp.float32)
        ).astype(jnp.bfloat16)

    def stage1(chunk):
        job, w = at(chunk)
        copies[chunk, 0].wait_recv()
        add(job, w, z_up, 0, cut(chunk), z1_up)
        copies[chunk, 2] = start(
            partial.at[job, part(z_up), w], z2_up.at[job, :, w], send.at[chunk, 2], recv.at[chunk, 2], up
        )
        copies[chunk, 1].wait_recv()
        add(job, w, z_down, cut(chunk), PIECE - cut(chunk), z1_down)
        copies[chunk, 3] = start(
            partial.at[job, part(z_down), w], z2_down.at[job, :, w], send.at[chunk, 3], recv.at[chunk, 3], down
        )

    def ring_sum(chunk):
        job, w = at(chunk)
        copies[chunk, 2].wait_recv()
        copies[chunk, 3].wait_recv()
        return (
            partial[job, part(z), w].astype(jnp.float32)
            + z2_up[job, :, w].astype(jnp.float32)
            + z2_down[job, :, w].astype(jnp.float32)
        ).astype(jnp.bfloat16)

    def stage2(chunk):
        job, w = at(chunk)
        mine[job, :, w] = ring_sum(chunk)
        copies[chunk, 4] = start(
            mine.at[job, :, w], other.at[job, :, w], send.at[chunk, 4], recv.at[chunk, 4], far
        )

    def same(chunk, lines, index, device, of=None):
        copies[chunk, index] = start(
            full(chunk, lines, of), full(chunk, lines, of), send.at[chunk, index], recv.at[chunk, index], device
        )

    def both(chunk, lines, index):
        same(chunk, lines, index, sibling)
        if chunk in CROSSED:
            same(chunk, lines, {7: 14, 9: 15, 11: 16, 12: 17}[index], far)

    def stage3(chunk):
        job, w = at(chunk)
        if chunk in CROSSED:
            total = ring_sum(chunk)
        else:
            copies[chunk, 4].wait_recv()
            total = mine[job, :, w].astype(jnp.float32) + other[job, :, w].astype(jnp.float32)
        full(chunk, span(core, z))[...] = total.astype(jnp.bfloat16)
        same(chunk, span(core, z), 5, up)
        same(chunk, span(core, z), 6, down)
        both(chunk, span(core, z), 7)

    def stage4(chunk):
        copies[chunk, 5].wait_recv()
        same(chunk, span(core, z_down, 0, cut(chunk)), 8, up)
        both(chunk, span(core, z_down), 9)
        copies[chunk, 6].wait_recv()
        same(chunk, span(core, z_up, cut(chunk), PIECE - cut(chunk)), 10, down)
        both(chunk, span(core, z_up), 11)

    def stage5(chunk):
        copies[chunk, 8].wait_recv()
        copies[chunk, 10].wait_recv()
        both(chunk, span(core, z_far), 12)

    def stage7(chunk):
        for index in (14, 15, 16, 17):
            copies[chunk, index].wait_recv()
        same(chunk, pl.ds(pl.multiple_of(core * HALF, 16), HALF), 18, sibling, 1 - side)

    def stage6(job):
        for chunk in range(len(CHUNKS)):
            if CHUNKS[chunk][0] == job:
                for index in (7, 9, 11, 12, 18):
                    if index < 18 or chunk in CROSSED:
                        copies[chunk, index].wait_recv()
        source = half_whole if job == 4 else whole.at[job]
        base = pair_energy[job]

        def body(step, carry):
            lines = pl.ds(pl.multiple_of(step * 128, 128), 128)
            plain = source[lines, :].astype(jnp.float32)
            swapped = jnp.transpose(source[:, lines]).astype(jnp.float32)
            gap = (base - virc[lines, 0:1]) - virr[0:1, :]
            value = (2.0 * plain - swapped) / gap
            if job == 4:
                a = lax.broadcasted_iota(jnp.int32, (128, NVIR), 0) + step * 128
                b = lax.broadcasted_iota(jnp.int32, (128, NVIR), 1)
                crossed = (a >= HALF).astype(jnp.int32) + (b >= HALF).astype(jnp.int32)
                value = jnp.where((crossed + turned) % 2 == 0, value, 0.0)
            amp[job, lines, :] = value.astype(jnp.bfloat16)
            return carry

        lax.fori_loop(0, NVIR // 128, body, 0, unroll=True)
        apply(job, first_side[job])

    def stage8(job):
        apply(job, 1 - first_side[job])

    first_side = (0, 1, 0, 0, 1)

    def apply(job, side):
        if side == 0:
            acc[left[job]] = acc[left[job]] + lax.dot_general(
                rows[right[job], own_part, :], amp[job], (((1,), (1,)), ((), ())), preferred_element_type=jnp.float32
            )
        else:
            acc[right[job]] = acc[right[job]] + jnp.dot(
                rows[left[job], own_part, :], amp[job], preferred_element_type=jnp.float32
            )

    halves = (pl.ds(0, ROWS // 2), pl.ds(ROWS // 2, ROWS // 2))

    def give_back(slot, device):
        index = slot - 1
        for h, lines in enumerate(halves):
            back_out[index, lines, :] = acc[slot, lines, :].astype(jnp.bfloat16)
            copies[slot, h] = start(
                back_out.at[index, lines], back_in.at[index, lines],
                b_send.at[4 + 2 * index + h], b_recv.at[4 + 2 * index + h], device,
            )

    own()
    stage0(1)
    next_part(0)
    stage0(2)
    stage0(0)
    stage1(1)
    next_part(1)
    stage1(2)
    stage0(3)
    stage1(0)
    next_part(2)
    stage2(2)
    prev()
    stage0(4)
    stage1(3)
    turn_prev()
    stage0(9)
    stage1(4)
    stage2(3)
    stage3(2)
    mate()
    stage1(9)
    turn_mate()
    stage0(6)
    stage2(4)
    stage0(7)
    stage4(2)
    stage0(5)
    stage3(3)
    stage1(6)
    stage3(4)
    stage1(7)
    stage2(9)
    stage4(3)
    stage9(5)
    stage4(4)
    stage0(8)
    stage2(7)
    stage3(9)
    stage5(3)
    stage1(5)
    stage2(1)
    stage5(4)
    stage1(8)
    stage5(2)
    stage2(6)
    stage4(9)
    stage3(5)
    stage3(7)
    stage6(1)
    stage2(8)
    stage5(9)
    stage4(5)
    stage3(6)
    stage6(4)
    give_back(NEXT, above)
    stage3(8)
    stage5(5)
    stage4(7)
    stage4(6)
    stage8(1)
    stage2(0)
    stage4(8)
    stage7(5)
    stage5(6)
    stage5(7)
    stage3(1)
    stage8(4)
    stage5(8)
    stage6(2)
    stage6(3)
    give_back(MATE, giver)
    stage8(3)
    give_back(PREV, below)
    stage3(0)
    stage4(1)
    stage5(1)
    stage8(2)
    stage4(0)
    stage5(0)
    stage6(0)
    stores = []
    for h, lines in enumerate(halves):
        for slot in (NEXT, PREV, MATE):
            copies[slot, h].wait_recv()
        total = acc[OWN, lines, :] + back_in[0, lines, :].astype(jnp.float32)
        total = total + back_in[1, lines, :].astype(jnp.float32) + back_in[2, lines, :].astype(jnp.float32)
        result[lines, :] = total.astype(jnp.bfloat16)
        stores.append(pltpu.make_async_copy(result.at[lines], out.at[lines], small.at[5 + h]))
        stores[h].start()
    for store in stores:
        store.wait()
    for copy in started:
        copy.wait_send()


def on_device(b_rows, aux_count, occ_pick, eps_occ, eps_vir):
    bf16, f32 = jnp.bfloat16, jnp.float32
    hbm = pl.BlockSpec(memory_space=pl.ANY)
    dma = pltpu.SemaphoreType.DMA
    gamma = pl.pallas_call(
        kernel,
        out_shape=jax.ShapeDtypeStruct((ROWS, NVIR), bf16),
        in_specs=[hbm] * 5,
        out_specs=hbm,
        scratch_shapes=[
            pltpu.SMEM((1,), jnp.int32),
            pltpu.SMEM((8,), jnp.int32),
            pltpu.SMEM((100,), f32),
            pltpu.VMEM((NVIR,), f32),
            dma((7,)),
            pltpu.VMEM((4, 2 * ROWS, NVIR), bf16),
            pltpu.VMEM((3, NVIR, 2 * ROWS), bf16),
            pltpu.VMEM((4, ROWS, NVIR), f32),
            pltpu.VMEM((JOBS, NVIR, NVIR), bf16),
            pltpu.VMEM((NVIR, 128), f32),
            pltpu.VMEM((8, NVIR), f32),
            pltpu.VMEM((JOBS, HALF, NVIR), bf16),
            pltpu.VMEM((JOBS - 1, NVIR, NVIR), bf16),
            pltpu.VMEM((NVIR, NVIR), bf16),
            pltpu.VMEM((JOBS, max(CUTS), NVIR), bf16),
            pltpu.VMEM((JOBS, max(CUTS), NVIR), bf16),
            pltpu.VMEM((JOBS, PIECE, NVIR), bf16),
            pltpu.VMEM((JOBS, PIECE, NVIR), bf16),
            pltpu.VMEM((JOBS, PIECE, NVIR), bf16),
            pltpu.VMEM((JOBS, PIECE, NVIR), bf16),
            pltpu.VMEM((max(1, len(CROSSED)), HALF, 256), bf16),
            pltpu.VMEM((3, ROWS, NVIR), bf16),
            pltpu.VMEM((3, ROWS, NVIR), bf16),
            pltpu.VMEM((ROWS, NVIR), bf16),
            dma((len(CHUNKS), 19)), dma((len(CHUNKS), 19)), dma((19,)), dma((19,)),
        ],
        compiler_params=pltpu.CompilerParams(
            collective_id=0, has_side_effects=True, vmem_limit_bytes=56 * 2**20
        ),
    )(aux_count, occ_pick, eps_occ, eps_vir, b_rows[:, 0, :])
    return gamma[:, None, :]


def solution(mesh):
    placed = (P("grp", "blk", None), P("grp"), P(), P(), P())
    return jax.shard_map(
        on_device, mesh=mesh, in_specs=placed, out_specs=P("grp", "blk", None), check_vma=False
    )
```

```python
import jax
import jax.numpy as jnp
from jax import lax
from jax.experimental import pallas as pl
from jax.experimental.pallas import tpu as pltpu
from jax.sharding import PartitionSpec as P

MESH = pl.DeviceIdType.MESH
ROWS, NVIR = 320, 896
HALF = NVIR // 2
PIECE = HALF // 4
CUTS = (64, 48)
PARTS = ((0, 256), (256, 256), (512, 384))
WINDOW = 512
OWN, NEXT, PREV, MATE = range(4)
JOBS = 5
CHUNKS = ((0, 0, 512), (0, 512, 384), (1, 0, 256), (1, 256, 256), (1, 512, 384), (2, 0, 512), (2, 512, 384), (3, 0, 512), (3, 512, 384), (4, 0, 512))
TURNS = (0, 1, 0, 1, 0, 0, 1, 0, 1, 1)
CROSSED = (5,)


def device_at(x, y, z, core):
    return (y * 2 + x % 2, z * 4 + (x // 2) * 2 + core)


def kernel(
    count_ref, pick_ref, occ_ref, vir_ref, b_ref, out,
    count, pick, occ, vir, small,
    rows, flipped, acc, amp, virc, virr, partial, whole, half_whole,
    z1_up, z1_down, z2_up, z2_down, mine, other, crossing, back_out, back_in, result,
    send, recv, b_send, b_recv,
):
    blk, grp = lax.axis_index("blk"), lax.axis_index("grp")
    y, lo = blk // 2, blk % 2
    z, core = grp // 4, grp % 2
    x = ((grp // 2) % 2) * 2 + lo
    y_up, y_down = (y + 1) % 4, (y + 3) % 4

    sibling = device_at(x, y, z, 1 - core)
    above, below = device_at(x, y_up, z, core), device_at(x, y_down, z, core)
    partner = device_at(x + 1 - 2 * lo, y, z, core)
    diagonal = device_at(x + 1 - 2 * lo, (y + 3 + 2 * lo) % 4, z, core)
    giver = device_at(x + 1 - 2 * lo, (y + lo) % 4, z, core)
    far = device_at((x + 2) % 4, y, z, core)
    up, down = device_at(x, y, (z + 1) % 4, core), device_at(x, y, (z + 3) % 4, core)

    own_part = pl.ds(pl.multiple_of(core * ROWS, 16), ROWS)
    started = []

    def remote(src, dst, sends, receives, device):
        copy = pltpu.make_async_remote_copy(
            src_ref=src, dst_ref=dst, send_sem=sends, recv_sem=receives,
            device_id=device, device_id_type=MESH,
        )
        started.append(copy)
        return copy

    def start(*where):
        copy = remote(*where)
        copy.start()
        return copy

    barrier = pltpu.get_barrier_semaphore()
    everyone = (sibling, above, below, partner, diagonal, far, up, down)
    for device in everyone:
        pl.semaphore_signal(barrier, inc=1, device_id=device, device_id_type=MESH)

    fetches = [
        pltpu.make_async_copy(src, dst, small.at[index])
        for index, (src, dst) in enumerate(
            (
                (b_ref, rows.at[OWN, own_part]), (count_ref, count), (vir_ref, vir),
                (pick_ref, pick), (occ_ref, occ),
            )
        )
    ]
    for fetch in fetches:
        fetch.start()

    half_whole[...] = jnp.zeros_like(half_whole)
    acc[...] = jnp.zeros_like(acc)

    fetches[0].wait()
    fetches[1].wait()
    line = lax.broadcasted_iota(jnp.int32, (ROWS, NVIR), 0)
    live = jnp.where(line < count[0], rows[OWN, own_part, :].astype(jnp.float32), 0.0)
    rows[OWN, own_part, :] = live.astype(jnp.bfloat16)

    pl.semaphore_wait(barrier, len(everyone))

    everything = pl.ds(0, NVIR)

    def spread(slot, columns, index, device):
        return start(
            rows.at[OWN, own_part, columns], rows.at[slot, own_part, columns],
            b_send.at[index], b_recv.at[index], device,
        )

    def pass_on(slot, columns, index):
        return start(
            rows.at[slot, own_part, columns], rows.at[slot, own_part, columns],
            b_send.at[index], b_recv.at[index], sibling,
        )

    def to_partner(columns, index):
        return remote(
            rows.at[(1 - lo) * NEXT, own_part, columns], rows.at[MATE, own_part, columns],
            b_send.at[index], b_recv.at[index], partner,
        )

    copies = {}
    pieces = range(len(PARTS))
    copies["own"] = spread(OWN, everything, 0, sibling)
    for i in pieces:
        copies["next", i] = spread(NEXT, pl.ds(*PARTS[i]), 10 + i, below)
    copies["prev"] = spread(PREV, everything, 1, above)
    for i in pieces:
        copies["mate", i] = to_partner(pl.ds(*PARTS[i]), 16 + i)

    @pl.when(lo == 1)
    def _():
        for i in pieces:
            copies["mate", i].start()

    for fetch in fetches[2:]:
        fetch.wait()
    virc[...] = jnp.transpose(jnp.broadcast_to(vir[...].reshape(1, NVIR), (128, NVIR)))
    virr[...] = jnp.broadcast_to(vir[...].reshape(1, NVIR), (8, NVIR))

    def energy(position):
        return occ[pick[position]]

    e_own = energy(blk)
    e_next = energy(y_up * 2 + lo)
    e_prev = energy(y_down * 2 + lo)
    e_mate = energy(((y + lo) % 4) * 2 + 1 - lo)
    pair_energy = (e_own + e_own, e_own + e_next, e_mate + e_own, e_mate + e_prev, e_prev + e_next)
    left = (OWN, OWN, MATE, MATE, PREV)
    right = (OWN, NEXT, OWN, PREV, NEXT)
    turned = y // 2

    def span(which, piece, first=0, size=PIECE):
        return pl.ds(pl.multiple_of(which * HALF + piece * PIECE + first, 16), size)

    def part(piece, first=0, size=PIECE):
        return pl.ds(pl.multiple_of(piece * PIECE + first, 16), size)

    z_up, z_down, z_far = (z + 1) % 4, (z + 3) % 4, (z + 2) % 4
    flip = (core + turned) % 2
    window = pl.ds(pl.multiple_of(flip * (NVIR - WINDOW), 128), WINDOW)

    side = x // 2

    def at(chunk, of=None):
        job, begin, size = CHUNKS[chunk]
        if chunk not in CROSSED:
            return job, pl.ds(begin, size)
        if of is None:
            of = side
        return job, pl.ds(pl.multiple_of(begin + of * (size // 2), 128), size // 2)

    def cut(chunk):
        return CUTS[TURNS[chunk]]

    def full(chunk, lines, of=None):
        job, w = at(chunk, of)
        if job == 4:
            begin = pl.multiple_of(flip * (NVIR - WINDOW) + w.start, 128)
            return half_whole.at[lines, pl.ds(begin, w.size)]
        return whole.at[job, lines, w]

    def turn(slot, index):
        def body(step, carry):
            lines = pl.ds(pl.multiple_of(step * 128, 128), 128)
            flipped[index, :, lines] = jnp.transpose(rows[slot, lines, :])
            return carry

        lax.fori_loop(0, 2 * ROWS // 128, body, 0, unroll=True)

    flip_index = (0, 0, 1, 1, 2)
    arrived = set()

    def need(*names):
        for name in names:
            if name not in arrived:
                arrived.add(name)
                copies[name].wait_recv()

    def own():
        copies["own"].wait_recv()
        turn(OWN, 0)

    def next_part(i):
        copies["next", i].wait_recv()
        copies["next on", i] = pass_on(NEXT, pl.ds(*PARTS[i]), 13 + i)
        pl.when(lo == 0)(copies["mate", i].start)

    def prev():
        copies["prev"].wait_recv()
        copies["prev on"] = pass_on(PREV, everything, 2)

    def turn_prev():
        need("prev on")
        turn(PREV, 2)

    def mate():
        for i in pieces:
            copies["mate", i].wait_recv()
        copies["mate on"] = pass_on(MATE, everything, 3)

    def turn_mate():
        copies["mate on"].wait_recv()
        turn(MATE, 1)

    def stage0(chunk):
        job, begin, size = CHUNKS[chunk]
        w = pl.ds(begin, size)
        if job in (1, 4):
            for i in pieces:
                if job == 4 or PARTS[i][0] < begin + size:
                    need(("next on", i))
        if job == 3:
            need("prev on")
        lhs = flipped[flip_index[job], pl.ds(pl.multiple_of(core * HALF, 16), HALF), :]
        rhs = rows[right[job], :, window] if job == 4 else rows[right[job], :, w]
        partial[job, :, w] = jnp.dot(lhs, rhs, preferred_element_type=jnp.float32).astype(jnp.bfloat16)
        if chunk in CROSSED:
            copies[chunk, 13] = start(
                partial.at[job, :, at(chunk, 1 - side)[1]], crossing.at[CROSSED.index(chunk)],
                send.at[chunk, 13], recv.at[chunk, 13], far,
            )
        else:
            into_ring(chunk)

    def stage9(chunk):
        job, w = at(chunk)
        copies[chunk, 13].wait_recv()
        partial[job, :, w] = (
            partial[job, :, w].astype(jnp.float32) + crossing[CROSSED.index(chunk)].astype(jnp.float32)
        ).astype(jnp.bfloat16)
        into_ring(chunk)

    def into_ring(chunk):
        job, w = at(chunk)
        copies[chunk, 0] = start(
            partial.at[job, part(z_far, 0, cut(chunk)), w], z1_up.at[job, pl.ds(0, cut(chunk)), w],
            send.at[chunk, 0], recv.at[chunk, 0], up,
        )
        copies[chunk, 1] = start(
            partial.at[job, part(z_far, cut(chunk), PIECE - cut(chunk)), w],
            z1_down.at[job, pl.ds(0, PIECE - cut(chunk)), w],
            send.at[chunk, 1], recv.at[chunk, 1], down,
        )

    def add(job, w, piece, begin, size, arrived):
        where = part(piece, begin, size)
        partial[job, where, w] = (
            partial[job, where, w].astype(jnp.float32) + arrived[job, 0:size, w].astype(jnp.float32)
        ).astype(jnp.bfloat16)

    def stage1(chunk):
        job, w = at(chunk)
        copies[chunk, 0].wait_recv()
        add(job, w, z_up, 0, cut(chunk), z1_up)
        copies[chunk, 2] = start(
            partial.at[job, part(z_up), w], z2_up.at[job, :, w], send.at[chunk, 2], recv.at[chunk, 2], up
        )
        copies[chunk, 1].wait_recv()
        add(job, w, z_down, cut(chunk), PIECE - cut(chunk), z1_down)
        copies[chunk, 3] = start(
            partial.at[job, part(z_down), w], z2_down.at[job, :, w], send.at[chunk, 3], recv.at[chunk, 3], down
        )

    def ring_sum(chunk):
        job, w = at(chunk)
        copies[chunk, 2].wait_recv()
        copies[chunk, 3].wait_recv()
        return (
            partial[job, part(z), w].astype(jnp.float32)
            + z2_up[job, :, w].astype(jnp.float32)
            + z2_down[job, :, w].astype(jnp.float32)
        ).astype(jnp.bfloat16)

    def stage2(chunk):
        job, w = at(chunk)
        mine[job, :, w] = ring_sum(chunk)
        copies[chunk, 4] = start(
            mine.at[job, :, w], other.at[job, :, w], send.at[chunk, 4], recv.at[chunk, 4], far
        )

    def same(chunk, lines, index, device, of=None):
        copies[chunk, index] = start(
            full(chunk, lines, of), full(chunk, lines, of), send.at[chunk, index], recv.at[chunk, index], device
        )

    def both(chunk, lines, index):
        same(chunk, lines, index, sibling)
        if chunk in CROSSED:
            same(chunk, lines, {7: 14, 9: 15, 11: 16, 12: 17}[index], far)

    def stage3(chunk):
        job, w = at(chunk)
        if chunk in CROSSED:
            total = ring_sum(chunk)
        else:
            copies[chunk, 4].wait_recv()
            total = mine[job, :, w].astype(jnp.float32) + other[job, :, w].astype(jnp.float32)
        full(chunk, span(core, z))[...] = total.astype(jnp.bfloat16)
        same(chunk, span(core, z), 5, up)
        same(chunk, span(core, z), 6, down)
        both(chunk, span(core, z), 7)

    def stage4(chunk):
        copies[chunk, 5].wait_recv()
        same(chunk, span(core, z_down, 0, cut(chunk)), 8, up)
        both(chunk, span(core, z_down), 9)
        copies[chunk, 6].wait_recv()
        same(chunk, span(core, z_up, cut(chunk), PIECE - cut(chunk)), 10, down)
        both(chunk, span(core, z_up), 11)

    def stage5(chunk):
        copies[chunk, 8].wait_recv()
        copies[chunk, 10].wait_recv()
        both(chunk, span(core, z_far), 12)

    def stage7(chunk):
        for index in (14, 15, 16, 17):
            copies[chunk, index].wait_recv()
        same(chunk, pl.ds(pl.multiple_of(core * HALF, 16), HALF), 18, sibling, 1 - side)

    def stage6(job):
        for chunk in range(len(CHUNKS)):
            if CHUNKS[chunk][0] == job:
                for index in (7, 9, 11, 12, 18):
                    if index < 18 or chunk in CROSSED:
                        copies[chunk, index].wait_recv()
        source = half_whole if job == 4 else whole.at[job]
        base = pair_energy[job]

        def body(step, carry):
            lines = pl.ds(pl.multiple_of(step * 128, 128), 128)
            plain = source[lines, :].astype(jnp.float32)
            swapped = jnp.transpose(source[:, lines]).astype(jnp.float32)
            gap = (base - virc[lines, 0:1]) - virr[0:1, :]
            value = (2.0 * plain - swapped) / gap
            if job == 4:
                a = lax.broadcasted_iota(jnp.int32, (128, NVIR), 0) + step * 128
                b = lax.broadcasted_iota(jnp.int32, (128, NVIR), 1)
                crossed = (a >= HALF).astype(jnp.int32) + (b >= HALF).astype(jnp.int32)
                value = jnp.where((crossed + turned) % 2 == 0, value, 0.0)
            amp[job, lines, :] = value.astype(jnp.bfloat16)
            return carry

        lax.fori_loop(0, NVIR // 128, body, 0, unroll=True)
        if job == 3:
            for h, lines in enumerate(halves):
                apply(job, first_side[job], lines)
                give_half(MATE, h, giver)
        else:
            apply(job, first_side[job])

    def stage8(job):
        apply(job, 1 - first_side[job])

    first_side = (0, 1, 0, 0, 1)

    def apply(job, side, lines=pl.ds(0, ROWS)):
        mine_here = pl.ds(pl.multiple_of(core * ROWS + lines.start, 16), lines.size)
        if side == 0:
            acc[left[job], lines, :] = acc[left[job], lines, :] + lax.dot_general(
                rows[right[job], mine_here, :], amp[job], (((1,), (1,)), ((), ())),
                preferred_element_type=jnp.float32,
            )
        else:
            acc[right[job], lines, :] = acc[right[job], lines, :] + jnp.dot(
                rows[left[job], mine_here, :], amp[job], preferred_element_type=jnp.float32
            )

    halves = (pl.ds(0, ROWS // 2), pl.ds(ROWS // 2, ROWS // 2))

    def give_half(slot, h, device):
        index, lines = slot - 1, halves[h]
        back_out[index, lines, :] = acc[slot, lines, :].astype(jnp.bfloat16)
        copies[slot, h] = start(
            back_out.at[index, lines], back_in.at[index, lines],
            b_send.at[4 + 2 * index + h], b_recv.at[4 + 2 * index + h], device,
        )

    def give_back(slot, device):
        for h in range(len(halves)):
            give_half(slot, h, device)

    own()
    stage0(1)
    next_part(0)
    stage0(2)
    stage0(0)
    stage1(1)
    next_part(1)
    stage1(2)
    stage0(3)
    stage1(0)
    next_part(2)
    stage2(2)
    prev()
    stage0(4)
    stage1(3)
    turn_prev()
    stage0(9)
    stage1(4)
    stage2(3)
    stage3(2)
    mate()
    stage1(9)
    turn_mate()
    stage0(6)
    stage2(4)
    stage0(7)
    stage4(2)
    stage0(5)
    stage3(3)
    stage1(6)
    stage3(4)
    stage1(7)
    stage2(9)
    stage4(3)
    stage9(5)
    stage4(4)
    stage0(8)
    stage2(7)
    stage3(9)
    stage5(3)
    stage1(5)
    stage2(1)
    stage5(4)
    stage1(8)
    stage5(2)
    stage2(6)
    stage4(9)
    stage3(5)
    stage3(7)
    stage6(1)
    stage2(8)
    stage5(9)
    stage4(5)
    stage3(6)
    stage6(4)
    give_back(NEXT, above)
    stage3(8)
    stage5(5)
    stage4(7)
    stage4(6)
    stage8(1)
    stage2(0)
    stage4(8)
    stage7(5)
    stage5(6)
    stage5(7)
    stage3(1)
    stage5(8)
    stage8(4)
    stage6(2)
    stage6(3)
    stage8(3)
    give_back(PREV, below)
    stage3(0)
    stage4(1)
    stage5(1)
    stage8(2)
    stage4(0)
    stage5(0)
    stage6(0)

    stores = []
    for h, lines in enumerate(halves):
        for slot in (NEXT, PREV, MATE):
            copies[slot, h].wait_recv()
        total = acc[OWN, lines, :] + back_in[0, lines, :].astype(jnp.float32)
        total = total + back_in[1, lines, :].astype(jnp.float32) + back_in[2, lines, :].astype(jnp.float32)
        result[lines, :] = total.astype(jnp.bfloat16)
        stores.append(pltpu.make_async_copy(result.at[lines], out.at[lines], small.at[5 + h]))
        stores[h].start()
    for store in stores:
        store.wait()
    for copy in started:
        copy.wait_send()


def on_device(b_rows, aux_count, occ_pick, eps_occ, eps_vir):
    bf16, f32 = jnp.bfloat16, jnp.float32
    hbm = pl.BlockSpec(memory_space=pl.ANY)
    dma = pltpu.SemaphoreType.DMA
    gamma = pl.pallas_call(
        kernel,
        out_shape=jax.ShapeDtypeStruct((ROWS, NVIR), bf16),
        in_specs=[hbm] * 5,
        out_specs=hbm,
        scratch_shapes=[
            pltpu.SMEM((1,), jnp.int32),
            pltpu.SMEM((8,), jnp.int32),
            pltpu.SMEM((100,), f32),
            pltpu.VMEM((NVIR,), f32),
            dma((7,)),
            pltpu.VMEM((4, 2 * ROWS, NVIR), bf16),
            pltpu.VMEM((3, NVIR, 2 * ROWS), bf16),
            pltpu.VMEM((4, ROWS, NVIR), f32),
            pltpu.VMEM((JOBS, NVIR, NVIR), bf16),
            pltpu.VMEM((NVIR, 128), f32),
            pltpu.VMEM((8, NVIR), f32),
            pltpu.VMEM((JOBS, HALF, NVIR), bf16),
            pltpu.VMEM((JOBS - 1, NVIR, NVIR), bf16),
            pltpu.VMEM((NVIR, NVIR), bf16),
            pltpu.VMEM((JOBS, max(CUTS), NVIR), bf16),
            pltpu.VMEM((JOBS, max(CUTS), NVIR), bf16),
            pltpu.VMEM((JOBS, PIECE, NVIR), bf16),
            pltpu.VMEM((JOBS, PIECE, NVIR), bf16),
            pltpu.VMEM((JOBS, PIECE, NVIR), bf16),
            pltpu.VMEM((JOBS, PIECE, NVIR), bf16),
            pltpu.VMEM((max(1, len(CROSSED)), HALF, 256), bf16),
            pltpu.VMEM((3, ROWS, NVIR), bf16),
            pltpu.VMEM((3, ROWS, NVIR), bf16),
            pltpu.VMEM((ROWS, NVIR), bf16),
            dma((len(CHUNKS), 19)), dma((len(CHUNKS), 19)), dma((19,)), dma((19,)),
        ],
        compiler_params=pltpu.CompilerParams(
            collective_id=0, has_side_effects=True, vmem_limit_bytes=56 * 2**20
        ),
    )(aux_count, occ_pick, eps_occ, eps_vir, b_rows[:, 0, :])
    return gamma[:, None, :]


def solution(mesh):
    placed = (P("grp", "blk", None), P("grp"), P(), P(), P())
    return jax.shard_map(
        on_device, mesh=mesh, in_specs=placed, out_specs=P("grp", "blk", None), check_vma=False
    )
```

```python
import jax
import jax.numpy as jnp
from jax import lax
from jax.experimental import pallas as pl
from jax.experimental.pallas import tpu as pltpu
from jax.sharding import PartitionSpec as P

MESH = pl.DeviceIdType.MESH
ROWS, NVIR = 320, 896
HALF = NVIR // 2
PIECE = HALF // 4
CUTS = (64, 48)
PARTS = ((0, 256), (256, 256), (512, 384))
WINDOW = 512
OWN, NEXT, PREV, MATE = range(4)
JOBS = 5
CHUNKS = ((0, 0, 512), (0, 512, 384), (1, 0, 256), (1, 256, 256), (1, 512, 384), (2, 0, 512), (2, 512, 384), (3, 0, 512), (3, 512, 384), (4, 0, 512))
TURNS = (0, 1, 0, 1, 0, 0, 1, 0, 1, 1)
CROSSED = (5,)


def device_at(x, y, z, core):
    return (y * 2 + x % 2, z * 4 + (x // 2) * 2 + core)


def kernel(
    count_ref, pick_ref, occ_ref, vir_ref, b_ref, out,
    count, pick, occ, vir, small,
    rows, flipped, acc, amp, virc, virr, partial, whole, half_whole,
    z1_up, z1_down, z2_up, z2_down, mine, other, crossing, back_out, back_in, result,
    send, recv, b_send, b_recv,
):
    blk, grp = lax.axis_index("blk"), lax.axis_index("grp")
    y, lo = blk // 2, blk % 2
    z, core = grp // 4, grp % 2
    x = ((grp // 2) % 2) * 2 + lo
    y_up, y_down = (y + 1) % 4, (y + 3) % 4

    sibling = device_at(x, y, z, 1 - core)
    above, below = device_at(x, y_up, z, core), device_at(x, y_down, z, core)
    partner = device_at(x + 1 - 2 * lo, y, z, core)
    diagonal = device_at(x + 1 - 2 * lo, (y + 3 + 2 * lo) % 4, z, core)
    giver = device_at(x + 1 - 2 * lo, (y + lo) % 4, z, core)
    far = device_at((x + 2) % 4, y, z, core)
    up, down = device_at(x, y, (z + 1) % 4, core), device_at(x, y, (z + 3) % 4, core)

    own_part = pl.ds(pl.multiple_of(core * ROWS, 16), ROWS)
    started = []

    def remote(src, dst, sends, receives, device):
        copy = pltpu.make_async_remote_copy(
            src_ref=src, dst_ref=dst, send_sem=sends, recv_sem=receives,
            device_id=device, device_id_type=MESH,
        )
        started.append(copy)
        return copy

    def start(*where):
        copy = remote(*where)
        copy.start()
        return copy

    barrier = pltpu.get_barrier_semaphore()
    everyone = (sibling, above, below, partner, diagonal, far, up, down)
    for device in everyone:
        pl.semaphore_signal(barrier, inc=1, device_id=device, device_id_type=MESH)

    fetches = [
        pltpu.make_async_copy(src, dst, small.at[index])
        for index, (src, dst) in enumerate(
            (
                (b_ref, rows.at[OWN, own_part]), (count_ref, count), (vir_ref, vir),
                (pick_ref, pick), (occ_ref, occ),
            )
        )
    ]
    for fetch in fetches:
        fetch.start()

    half_whole[...] = jnp.zeros_like(half_whole)
    acc[...] = jnp.zeros_like(acc)

    fetches[0].wait()
    fetches[1].wait()
    line = lax.broadcasted_iota(jnp.int32, (ROWS, NVIR), 0)
    live = jnp.where(line < count[0], rows[OWN, own_part, :].astype(jnp.float32), 0.0)
    rows[OWN, own_part, :] = live.astype(jnp.bfloat16)

    pl.semaphore_wait(barrier, len(everyone))

    everything = pl.ds(0, NVIR)

    def spread(slot, columns, index, device):
        return start(
            rows.at[OWN, own_part, columns], rows.at[slot, own_part, columns],
            b_send.at[index], b_recv.at[index], device,
        )

    def pass_on(slot, columns, index):
        return start(
            rows.at[slot, own_part, columns], rows.at[slot, own_part, columns],
            b_send.at[index], b_recv.at[index], sibling,
        )

    def to_partner(columns, index):
        return remote(
            rows.at[(1 - lo) * NEXT, own_part, columns], rows.at[MATE, own_part, columns],
            b_send.at[index], b_recv.at[index], partner,
        )

    copies = {}
    pieces = range(len(PARTS))
    copies["own"] = spread(OWN, everything, 0, sibling)
    for i in pieces:
        copies["next", i] = spread(NEXT, pl.ds(*PARTS[i]), 10 + i, below)
    copies["prev"] = spread(PREV, everything, 1, above)
    for i in pieces:
        copies["mate", i] = to_partner(pl.ds(*PARTS[i]), 16 + i)

    @pl.when(lo == 1)
    def _():
        for i in pieces:
            copies["mate", i].start()

    for fetch in fetches[2:]:
        fetch.wait()
    virc[...] = jnp.transpose(jnp.broadcast_to(vir[...].reshape(1, NVIR), (128, NVIR)))
    virr[...] = jnp.broadcast_to(vir[...].reshape(1, NVIR), (8, NVIR))

    def energy(position):
        return occ[pick[position]]

    e_own = energy(blk)
    e_next = energy(y_up * 2 + lo)
    e_prev = energy(y_down * 2 + lo)
    e_mate = energy(((y + lo) % 4) * 2 + 1 - lo)
    pair_energy = (e_own + e_own, e_own + e_next, e_mate + e_own, e_mate + e_prev, e_prev + e_next)
    left = (OWN, OWN, MATE, MATE, PREV)
    right = (OWN, NEXT, OWN, PREV, NEXT)
    turned = y // 2

    def span(which, piece, first=0, size=PIECE):
        return pl.ds(pl.multiple_of(which * HALF + piece * PIECE + first, 16), size)

    def part(piece, first=0, size=PIECE):
        return pl.ds(pl.multiple_of(piece * PIECE + first, 16), size)

    z_up, z_down, z_far = (z + 1) % 4, (z + 3) % 4, (z + 2) % 4
    flip = (core + turned) % 2
    window = pl.ds(pl.multiple_of(flip * (NVIR - WINDOW), 128), WINDOW)

    side = x // 2

    def at(chunk, of=None):
        job, begin, size = CHUNKS[chunk]
        if chunk not in CROSSED:
            return job, pl.ds(begin, size)
        if of is None:
            of = side
        return job, pl.ds(pl.multiple_of(begin + of * (size // 2), 128), size // 2)

    def cut(chunk):
        return CUTS[TURNS[chunk]]

    def full(chunk, lines, of=None):
        job, w = at(chunk, of)
        if job == 4:
            begin = pl.multiple_of(flip * (NVIR - WINDOW) + w.start, 128)
            return half_whole.at[lines, pl.ds(begin, w.size)]
        return whole.at[job, lines, w]

    def turn(slot, index):
        def body(step, carry):
            lines = pl.ds(pl.multiple_of(step * 128, 128), 128)
            flipped[index, :, lines] = jnp.transpose(rows[slot, lines, :])
            return carry

        lax.fori_loop(0, 2 * ROWS // 128, body, 0, unroll=True)

    flip_index = (0, 0, 1, 1, 2)
    arrived = set()

    def need(*names):
        for name in names:
            if name not in arrived:
                arrived.add(name)
                copies[name].wait_recv()

    def own():
        copies["own"].wait_recv()
        turn(OWN, 0)

    def next_part(i):
        copies["next", i].wait_recv()
        copies["next on", i] = pass_on(NEXT, pl.ds(*PARTS[i]), 13 + i)
        pl.when(lo == 0)(copies["mate", i].start)

    def prev():
        copies["prev"].wait_recv()
        copies["prev on"] = pass_on(PREV, everything, 2)

    def turn_prev():
        need("prev on")
        turn(PREV, 2)

    def mate():
        for i in pieces:
            copies["mate", i].wait_recv()
        copies["mate on"] = pass_on(MATE, everything, 3)

    def turn_mate():
        copies["mate on"].wait_recv()
        turn(MATE, 1)

    def stage0(chunk):
        job, begin, size = CHUNKS[chunk]
        w = pl.ds(begin, size)
        if job in (1, 4):
            for i in pieces:
                if job == 4 or PARTS[i][0] < begin + size:
                    need(("next on", i))
        if job == 3:
            need("prev on")
        lhs = flipped[flip_index[job], pl.ds(pl.multiple_of(core * HALF, 16), HALF), :]
        rhs = rows[right[job], :, window] if job == 4 else rows[right[job], :, w]
        partial[job, :, w] = jnp.dot(lhs, rhs, preferred_element_type=jnp.float32).astype(jnp.bfloat16)
        if chunk in CROSSED:
            copies[chunk, 13] = start(
                partial.at[job, :, at(chunk, 1 - side)[1]], crossing.at[CROSSED.index(chunk)],
                send.at[chunk, 13], recv.at[chunk, 13], far,
            )
        else:
            into_ring(chunk)

    def stage9(chunk):
        job, w = at(chunk)
        copies[chunk, 13].wait_recv()
        partial[job, :, w] = (
            partial[job, :, w].astype(jnp.float32) + crossing[CROSSED.index(chunk)].astype(jnp.float32)
        ).astype(jnp.bfloat16)
        into_ring(chunk)

    def into_ring(chunk):
        job, w = at(chunk)
        copies[chunk, 0] = start(
            partial.at[job, part(z_far, 0, cut(chunk)), w], z1_up.at[job, pl.ds(0, cut(chunk)), w],
            send.at[chunk, 0], recv.at[chunk, 0], up,
        )
        copies[chunk, 1] = start(
            partial.at[job, part(z_far, cut(chunk), PIECE - cut(chunk)), w],
            z1_down.at[job, pl.ds(0, PIECE - cut(chunk)), w],
            send.at[chunk, 1], recv.at[chunk, 1], down,
        )

    def add(job, w, piece, begin, size, arrived):
        where = part(piece, begin, size)
        partial[job, where, w] = (
            partial[job, where, w].astype(jnp.float32) + arrived[job, 0:size, w].astype(jnp.float32)
        ).astype(jnp.bfloat16)

    def stage1(chunk):
        job, w = at(chunk)
        copies[chunk, 0].wait_recv()
        add(job, w, z_up, 0, cut(chunk), z1_up)
        copies[chunk, 2] = start(
            partial.at[job, part(z_up), w], z2_up.at[job, :, w], send.at[chunk, 2], recv.at[chunk, 2], up
        )
        copies[chunk, 1].wait_recv()
        add(job, w, z_down, cut(chunk), PIECE - cut(chunk), z1_down)
        copies[chunk, 3] = start(
            partial.at[job, part(z_down), w], z2_down.at[job, :, w], send.at[chunk, 3], recv.at[chunk, 3], down
        )

    def ring_sum(chunk):
        job, w = at(chunk)
        copies[chunk, 2].wait_recv()
        copies[chunk, 3].wait_recv()
        return (
            partial[job, part(z), w].astype(jnp.float32)
            + z2_up[job, :, w].astype(jnp.float32)
            + z2_down[job, :, w].astype(jnp.float32)
        ).astype(jnp.bfloat16)

    def stage2(chunk):
        job, w = at(chunk)
        mine[job, :, w] = ring_sum(chunk)
        copies[chunk, 4] = start(
            mine.at[job, :, w], other.at[job, :, w], send.at[chunk, 4], recv.at[chunk, 4], far
        )

    def same(chunk, lines, index, device, of=None):
        copies[chunk, index] = start(
            full(chunk, lines, of), full(chunk, lines, of), send.at[chunk, index], recv.at[chunk, index], device
        )

    def both(chunk, lines, index):
        same(chunk, lines, index, sibling)
        if chunk in CROSSED:
            same(chunk, lines, {7: 14, 9: 15, 11: 16, 12: 17}[index], far)

    def stage3(chunk):
        job, w = at(chunk)
        if chunk in CROSSED:
            total = ring_sum(chunk)
        else:
            copies[chunk, 4].wait_recv()
            total = mine[job, :, w].astype(jnp.float32) + other[job, :, w].astype(jnp.float32)
        full(chunk, span(core, z))[...] = total.astype(jnp.bfloat16)
        same(chunk, span(core, z), 5, up)
        same(chunk, span(core, z), 6, down)
        both(chunk, span(core, z), 7)

    def stage4(chunk):
        copies[chunk, 5].wait_recv()
        same(chunk, span(core, z_down, 0, cut(chunk)), 8, up)
        both(chunk, span(core, z_down), 9)
        copies[chunk, 6].wait_recv()
        same(chunk, span(core, z_up, cut(chunk), PIECE - cut(chunk)), 10, down)
        both(chunk, span(core, z_up), 11)

    def stage5(chunk):
        copies[chunk, 8].wait_recv()
        copies[chunk, 10].wait_recv()
        both(chunk, span(core, z_far), 12)

    def stage7(chunk):
        for index in (14, 15, 16, 17):
            copies[chunk, index].wait_recv()
        same(chunk, pl.ds(pl.multiple_of(core * HALF, 16), HALF), 18, sibling, 1 - side)

    def stage6(job):
        for chunk in range(len(CHUNKS)):
            if CHUNKS[chunk][0] == job:
                for index in (7, 9, 11, 12, 18):
                    if index < 18 or chunk in CROSSED:
                        copies[chunk, index].wait_recv()
        source = half_whole if job == 4 else whole.at[job]
        base = pair_energy[job]

        def body(step, carry):
            lines = pl.ds(pl.multiple_of(step * 128, 128), 128)
            plain = source[lines, :].astype(jnp.float32)
            swapped = jnp.transpose(source[:, lines]).astype(jnp.float32)
            gap = (base - virc[lines, 0:1]) - virr[0:1, :]
            value = (2.0 * plain - swapped) / gap
            if job == 4:
                a = lax.broadcasted_iota(jnp.int32, (128, NVIR), 0) + step * 128
                b = lax.broadcasted_iota(jnp.int32, (128, NVIR), 1)
                crossed = (a >= HALF).astype(jnp.int32) + (b >= HALF).astype(jnp.int32)
                value = jnp.where((crossed + turned) % 2 == 0, value, 0.0)
            amp[job, lines, :] = value.astype(jnp.bfloat16)
            return carry

        lax.fori_loop(0, NVIR // 128, body, 0, unroll=True)
        if job == 3:
            for h, lines in enumerate(halves):
                apply(job, first_side[job], lines)
                give_half(MATE, h, giver)
        else:
            apply(job, first_side[job])

    def stage8(job):
        if job == 3:
            for h, lines in enumerate(halves):
                apply(job, 1 - first_side[job], lines)
                give_half(PREV, h, below)
        else:
            apply(job, 1 - first_side[job])

    first_side = (0, 1, 0, 0, 1)

    def apply(job, side, lines=pl.ds(0, ROWS)):
        mine_here = pl.ds(pl.multiple_of(core * ROWS + lines.start, 16), lines.size)
        if side == 0:
            acc[left[job], lines, :] = acc[left[job], lines, :] + lax.dot_general(
                rows[right[job], mine_here, :], amp[job], (((1,), (1,)), ((), ())),
                preferred_element_type=jnp.float32,
            )
        else:
            acc[right[job], lines, :] = acc[right[job], lines, :] + jnp.dot(
                rows[left[job], mine_here, :], amp[job], preferred_element_type=jnp.float32
            )

    halves = (pl.ds(0, ROWS // 2), pl.ds(ROWS // 2, ROWS // 2))

    def give_half(slot, h, device):
        index, lines = slot - 1, halves[h]
        back_out[index, lines, :] = acc[slot, lines, :].astype(jnp.bfloat16)
        copies[slot, h] = start(
            back_out.at[index, lines], back_in.at[index, lines],
            b_send.at[4 + 2 * index + h], b_recv.at[4 + 2 * index + h], device,
        )

    def give_back(slot, device):
        for h in range(len(halves)):
            give_half(slot, h, device)

    own()
    stage0(1)
    next_part(0)
    stage0(2)
    stage0(0)
    stage1(1)
    next_part(1)
    stage1(2)
    stage0(3)
    stage1(0)
    next_part(2)
    stage2(2)
    prev()
    stage0(4)
    stage1(3)
    turn_prev()
    stage0(9)
    stage1(4)
    stage2(3)
    stage3(2)
    mate()
    stage1(9)
    turn_mate()
    stage0(6)
    stage2(4)
    stage0(7)
    stage4(2)
    stage0(5)
    stage3(3)
    stage1(6)
    stage3(4)
    stage1(7)
    stage2(9)
    stage4(3)
    stage9(5)
    stage4(4)
    stage0(8)
    stage2(7)
    stage3(9)
    stage5(3)
    stage1(5)
    stage2(1)
    stage5(4)
    stage1(8)
    stage5(2)
    stage2(6)
    stage4(9)
    stage3(5)
    stage3(7)
    stage6(1)
    stage2(8)
    stage5(9)
    stage4(5)
    stage3(6)
    stage6(4)
    give_back(NEXT, above)
    stage3(8)
    stage5(5)
    stage4(7)
    stage4(6)
    stage8(1)
    stage2(0)
    stage4(8)
    stage7(5)
    stage5(6)
    stage5(7)
    stage3(1)
    stage5(8)
    stage8(4)
    stage6(2)
    stage6(3)
    stage8(3)
    stage3(0)
    stage4(1)
    stage5(1)
    stage8(2)
    stage4(0)
    stage5(0)
    stage6(0)

    stores = []
    for h, lines in enumerate(halves):
        for slot in (NEXT, PREV, MATE):
            copies[slot, h].wait_recv()
        total = acc[OWN, lines, :] + back_in[0, lines, :].astype(jnp.float32)
        total = total + back_in[1, lines, :].astype(jnp.float32) + back_in[2, lines, :].astype(jnp.float32)
        result[lines, :] = total.astype(jnp.bfloat16)
        stores.append(pltpu.make_async_copy(result.at[lines], out.at[lines], small.at[5 + h]))
        stores[h].start()
    for store in stores:
        store.wait()
    for copy in started:
        copy.wait_send()


def on_device(b_rows, aux_count, occ_pick, eps_occ, eps_vir):
    bf16, f32 = jnp.bfloat16, jnp.float32
    hbm = pl.BlockSpec(memory_space=pl.ANY)
    dma = pltpu.SemaphoreType.DMA
    gamma = pl.pallas_call(
        kernel,
        out_shape=jax.ShapeDtypeStruct((ROWS, NVIR), bf16),
        in_specs=[hbm] * 5,
        out_specs=hbm,
        scratch_shapes=[
            pltpu.SMEM((1,), jnp.int32),
            pltpu.SMEM((8,), jnp.int32),
            pltpu.SMEM((100,), f32),
            pltpu.VMEM((NVIR,), f32),
            dma((7,)),
            pltpu.VMEM((4, 2 * ROWS, NVIR), bf16),
            pltpu.VMEM((3, NVIR, 2 * ROWS), bf16),
            pltpu.VMEM((4, ROWS, NVIR), f32),
            pltpu.VMEM((JOBS, NVIR, NVIR), bf16),
            pltpu.VMEM((NVIR, 128), f32),
            pltpu.VMEM((8, NVIR), f32),
            pltpu.VMEM((JOBS, HALF, NVIR), bf16),
            pltpu.VMEM((JOBS - 1, NVIR, NVIR), bf16),
            pltpu.VMEM((NVIR, NVIR), bf16),
            pltpu.VMEM((JOBS, max(CUTS), NVIR), bf16),
            pltpu.VMEM((JOBS, max(CUTS), NVIR), bf16),
            pltpu.VMEM((JOBS, PIECE, NVIR), bf16),
            pltpu.VMEM((JOBS, PIECE, NVIR), bf16),
            pltpu.VMEM((JOBS, PIECE, NVIR), bf16),
            pltpu.VMEM((JOBS, PIECE, NVIR), bf16),
            pltpu.VMEM((max(1, len(CROSSED)), HALF, 256), bf16),
            pltpu.VMEM((3, ROWS, NVIR), bf16),
            pltpu.VMEM((3, ROWS, NVIR), bf16),
            pltpu.VMEM((ROWS, NVIR), bf16),
            dma((len(CHUNKS), 19)), dma((len(CHUNKS), 19)), dma((19,)), dma((19,)),
        ],
        compiler_params=pltpu.CompilerParams(
            collective_id=0, has_side_effects=True, vmem_limit_bytes=56 * 2**20
        ),
    )(aux_count, occ_pick, eps_occ, eps_vir, b_rows[:, 0, :])
    return gamma[:, None, :]


def solution(mesh):
    placed = (P("grp", "blk", None), P("grp"), P(), P(), P())
    return jax.shard_map(
        on_device, mesh=mesh, in_specs=placed, out_specs=P("grp", "blk", None), check_vma=False
    )
```
